512 devices in a mesh: inj: 4 (over y), blk: 128 (over z, x, core).
Axes of the slice: x: 4, y: 4, z: 16, core: 2. Of those that a mesh axis runs over, the one named last changes fastest.
Arguments:
- tile_values: bfloat16 [1536, 128, 128], P('blk'), may hold values from -0.3125 to 0.3125
- tile_row: int32 [1536], P('blk'), may hold values from 0 to 3
- tile_dest: int32 [1536, 1], P('blk'), may hold values from 0 to 6, as said below
- trans_block: int32 [128, 21], P('blk'), may hold values from 0 to 3
- inj_pores: int32 [256, 8192], P('inj', 'blk'), may hold values from 0 to 511
- final_weight: bfloat16 [256, 65536], P('inj', 'blk'), may hold values from -6 to 6
Outputs:
- sensitivity: bfloat16 [256, 65536], P('inj', 'blk')
- tile_gradient: bfloat16 [1536, 128, 128], P('blk', 'inj')
The draws below stay inside these ranges and needn't reach their ends.
Inputs may be any that keep to these rules, and one draw needn't show every extreme that they name: `tile_dest`: among the tiles of one index of blk, every value is named by at most 3 tiles, and 0 by exactly 3 tiles.
All inputs are finite; a program needn't handle non-finite values.
Results may differ from the reference program's by a relative error of at most 0.014.
Values may be sent and summed in bfloat16 or wider, within the bound.
A program may use at most 64 MiB of HBM per device.

```python
import math
import jax
import jax.numpy as jnp
import numpy as np
from jax import lax

BW = 128
SET_DEV = 64
DEG = 3
NEIGH = 6
STEPS = 4
BLK_DEV = 4
TILE_DEV = 12
CAP = 3
PORES_DEV = 512
INJ_DEV = 64
NB = 512
PORES = 65536
TILES = 1536
SETS = 256
N_INJ = 4
N_BLK = 128


def draw_tile_dest(key, part):

    def one_device(sub):
        first_key, second_key = jax.random.split(sub)
        order = jax.random.permutation(first_key, NEIGH * CAP).astype(jnp.int32)
        chosen = (order[:TILE_DEV - CAP] // CAP + 1).astype(jnp.int32)
        labels = jnp.concatenate([jnp.zeros((CAP,), jnp.int32), chosen])
        return jax.random.permutation(second_key, labels).astype(jnp.int32)
    keys = jax.random.split(jax.random.fold_in(key, 7), N_BLK)
    return jax.vmap(one_device)(keys).reshape(TILES, 1).astype(jnp.int32)


def with_ends(entries, stream_key, least, high):
    dims = entries.shape
    place = [jax.random.randint(jax.random.fold_in(stream_key, axis), (), 0, dims[axis]) for axis in range(len(dims))]
    entries = entries.at[tuple(place)].set(least)
    longest = dims.index(max(dims))
    place[longest] = (place[longest] + 1) % dims[longest]
    return entries.at[tuple(place)].set(high)


def levels(rng, dims, cuts, smallest, top_value):
    gain = 1.0
    for axis_at, shards_of in cuts:
        heights = jax.random.uniform(jax.random.fold_in(jax.random.fold_in(rng, 6), axis_at), (shards_of,), jnp.float32, smallest / len(cuts), top_value / len(cuts))
        gain = gain * jnp.repeat(jnp.exp(heights), dims[axis_at] // shards_of).reshape((-1,) + (1,) * (len(dims) - 1 - axis_at))
    return gain


def rank_table(number_of, skew):
    portions = [(1 << 20) // math.isqrt(rank ** skew) + 1 for rank in range(1, number_of + 1)]
    spread = 1 + sum(portions) // (1 << 30)
    return np.cumsum(np.array([max(1, weight // spread) for weight in portions]))


def ranked_ids(rng, shape, count, lean):
    grid = rank_table(count, lean)
    pick = jax.random.randint(jax.random.fold_in(rng, 1), shape, 0, int(grid[count - 1]))
    rank = jnp.searchsorted(jnp.asarray(grid, jnp.int32), pick, side="right")
    return jax.random.permutation(jax.random.fold_in(rng, 2), count)[rank].astype(jnp.int32)


def noise(rng, dims, spread, reach, shards=(), held_as=jnp.bfloat16):
    drawn = spread * jax.random.normal(rng, dims, jnp.float32)
    if shards:
        drawn = drawn * levels(rng, dims, shards, -0.22, 0.18)
    return jnp.clip(drawn, -reach, reach).astype(held_as)


def setup_inputs(seed: int = 0) -> dict:
    seeds = jax.random.split(jax.random.key(seed), 7)
    return {
        "tile_values": noise(seeds[0], (TILES, BW, BW), (DEG * BW) ** -0.5, 0.3125, ((0, 128),)),
        "tile_row": with_ends(ranked_ids(seeds[1], (TILES,), BLK_DEV, 2), jax.random.fold_in(seeds[1], 3), 0, BLK_DEV - 1).astype(jnp.int32),
        "tile_dest": draw_tile_dest(jax.random.fold_in(seeds[6], 71), 0),
        "trans_block": with_ends(jax.random.randint(seeds[3], (N_BLK, (NEIGH + 1) * CAP), 0, BLK_DEV), jax.random.fold_in(seeds[3], 1), 0, BLK_DEV - 1).astype(jnp.int32),
        "inj_pores": with_ends(jax.random.randint(seeds[4], (SETS, INJ_DEV * N_BLK), 0, PORES_DEV), jax.random.fold_in(seeds[4], 1), 0, PORES_DEV - 1).astype(jnp.int32),
        "final_weight": noise(seeds[5], (SETS, PORES), 1.0, 6.0, ((0, 4), (1, 128))),
    }


def reference(tile_values, tile_row, tile_dest, trans_block, inj_pores, final_weight):
    highest = lax.Precision.HIGHEST
    slot_ids = jnp.arange(NEIGH + 1, dtype=jnp.int32)
    half_ids = ((slot_ids + 1) // 2).astype(jnp.int32)
    offsets = jnp.where(slot_ids % 2 == 1, half_ids, -half_ids).astype(jnp.int32)
    targets = tile_dest.reshape(N_BLK, TILE_DEV).astype(jnp.int32)
    rows_local = tile_row.reshape(N_BLK, TILE_DEV).astype(jnp.int32)
    ordinal = jnp.arange(TILE_DEV, dtype=jnp.int32)
    earlier = ordinal[:, None] > ordinal[None, :]
    position = jnp.sum(((targets[:, :, None] == targets[:, None, :]) & earlier[None]).astype(jnp.int32), axis=2).astype(jnp.int32)
    owners = jnp.arange(N_BLK, dtype=jnp.int32)[:, None]
    dest_dev = ((owners + offsets[targets]) % N_BLK).astype(jnp.int32)
    local_col = trans_block[dest_dev, targets * CAP + position].astype(jnp.int32)
    col_glob = (dest_dev * BLK_DEV + local_col).astype(jnp.int32)
    row_glob = (owners * BLK_DEV + rows_local).astype(jnp.int32)
    tiles = tile_values.reshape(N_BLK, TILE_DEV, BW, BW)

    entry_dev = (jnp.arange(INJ_DEV * N_BLK, dtype=jnp.int32) // INJ_DEV).astype(jnp.int32)
    pore_ids = (entry_dev[None, :] * PORES_DEV + inj_pores).astype(jnp.int32)
    set_ids = jnp.arange(SETS, dtype=jnp.int32)[:, None]
    initial = jnp.zeros((SETS, PORES), jnp.float32).at[set_ids, pore_ids].add(1.0)
    initial = initial.astype(jnp.bfloat16).reshape(SETS, NB, BW)

    def advance(state):
        def one_device(pieces):
            tile_set, row_set, col_set = pieces
            fetched = state[:, col_set].astype(jnp.float32)
            contrib = jnp.einsum("sib,iab->sia", fetched, tile_set.astype(jnp.float32), precision=highest)
            row_hot = (row_set[:, None] == jnp.arange(BLK_DEV, dtype=jnp.int32)[None, :]).astype(jnp.float32)
            return jnp.einsum("sia,ic->sca", contrib, row_hot, precision=highest).astype(jnp.bfloat16)
        result = lax.map(one_device, (tiles, rows_local, col_glob))
        return jnp.transpose(result, (1, 0, 2, 3)).reshape(SETS, NB, BW)

    states = [initial]
    for timestep in range(STEPS - 1):
        states.append(advance(states[-1]))

    def retreat(adjoint):
        def add_device(total, pieces):
            tile_set, row_set, col_set = pieces
            rows_now = adjoint[:, row_set].astype(jnp.float32)
            term = jnp.einsum("sia,iab->sib", rows_now, tile_set.astype(jnp.float32), precision=highest)
            term = lax.optimization_barrier(term.astype(jnp.bfloat16)).astype(jnp.float32)
            return total.at[:, col_set].add(term), None
        total, unused = lax.scan(add_device, jnp.zeros((SETS, NB, BW), jnp.float32), (tiles, row_glob, col_glob))
        return total.astype(jnp.bfloat16)

    adjoints = [None] * (STEPS + 1)
    adjoints[STEPS] = final_weight.reshape(SETS, NB, BW)
    for timestep in reversed(range(STEPS)):
        adjoints[timestep] = retreat(adjoints[timestep + 1])

    def grad_device(pieces):
        row_set, col_set = pieces
        accum = jnp.zeros((N_INJ, TILE_DEV, BW, BW), jnp.float32)
        for timestep in range(STEPS):
            rows_now = adjoints[timestep + 1][:, row_set].astype(jnp.float32).reshape(N_INJ, SET_DEV, TILE_DEV, BW)
            cols_now = states[timestep][:, col_set].astype(jnp.float32).reshape(N_INJ, SET_DEV, TILE_DEV, BW)
            accum = accum + jnp.einsum("gsia,gsib->giab", rows_now, cols_now, precision=highest)
        partial_sum = lax.optimization_barrier((accum * (1.0 / SET_DEV)).astype(jnp.bfloat16)).astype(jnp.float32)
        return jnp.sum(partial_sum, axis=0).astype(jnp.bfloat16)

    tile_gradient = lax.map(grad_device, (row_glob, col_glob)).reshape(TILES, BW, BW)
    sensitivity = adjoints[0].reshape(SETS, PORES)
    return (sensitivity, tile_gradient)
```

```python
import functools

import jax
import jax.numpy as jnp
from jax import lax
from jax.experimental import pallas as pl
from jax.experimental.pallas import tpu as pltpu
from jax.sharding import PartitionSpec as P

NEIGH = 6
STEPS = 4
CAP = 3
SLOTS = (NEIGH + 1) * CAP
HALVES = 2
MESH = pl.DeviceIdType.MESH
F32 = jnp.float32
BF16 = jnp.bfloat16


def offset_of(slot):
    amount = (slot + 1) // 2
    return amount if slot % 2 == 1 else -amount


def dot_nt(x, y):
    return lax.dot_general(x, y, (((1,), (1,)), ((), ())), preferred_element_type=F32)


def dot_nn(x, y):
    return lax.dot_general(x, y, (((1,), (0,)), ((), ())), preferred_element_type=F32)


def sweep(
    n_inj, n_blk, blocks, tiles_dev, row_in, dest_in, trans_in, tiles_hbm, pores_hbm, weight_hbm,
    sens_ref, grad_ref, tiles, pores, state, adj, adj_t, terms, fsend, bsend, brecv, gsend, grecv,
    slot_s, tile_s, rowmask, transmask, in_sem, fs_sem, fr_sem, bs_sem, br_sem, gs_sem, gr_sem, *fetched,
):
    me_i, me_b = lax.axis_index("inj"), lax.axis_index("blk")
    sets = pores.shape[0]
    hs = sets // HALVES
    width = tiles.shape[-1]
    portion = width // n_inj

    def at_blk(distance):
        return (me_i, lax.rem(me_b + (distance + n_blk), n_blk))

    def at_inj(distance):
        return lax.rem(me_i + distance, n_inj)

    barrier = pltpu.get_barrier_semaphore()
    for j in range(1, NEIGH + 1):
        pl.semaphore_signal(barrier, inc=1, device_id=at_blk(offset_of(j)), device_id_type=MESH)
    for o in range(1, n_inj):
        pl.semaphore_signal(barrier, inc=1, device_id=(at_inj(o), me_b), device_id_type=MESH)

    loads = [
        pltpu.make_async_copy(pores_hbm, pores, in_sem.at[0]),
        pltpu.make_async_copy(tiles_hbm, tiles, in_sem.at[1]),
    ]
    for c in range(blocks):
        loads.append(
            pltpu.make_async_copy(
                weight_hbm.at[:, pl.ds(c * width, width)],
                adj.at[c, pl.ds((STEPS - 1) * sets, sets)],
                in_sem.at[2 + c],
            )
        )
    for load in loads:
        load.start()

    dests = [dest_in[i, 0] for i in range(tiles_dev)]
    slots = []
    for i in range(tiles_dev):
        earlier = jnp.int32(0)
        for e in range(i):
            earlier = earlier + jnp.where(dests[e] == dests[i], 1, 0)
        slots.append(dests[i] * CAP + earlier)
        slot_s[i] = slots[i]
    for n in range(SLOTS):
        user = jnp.int32(tiles_dev)
        for i in range(tiles_dev):
            user = jnp.where(slots[i] == n, i, user)
        tile_s[n] = user
    for i in range(tiles_dev):
        for r in range(blocks):
            rowmask[i * blocks + r] = jnp.where(row_in[i] == r, 1.0, 0.0).astype(F32)
    for n in range(SLOTS):
        for c in range(blocks):
            transmask[n * blocks + c] = jnp.where(trans_in[0, n] == c, 1.0, 0.0).astype(F32)
    terms[tiles_dev] = jnp.zeros_like(terms[tiles_dev])

    def f_copy(t, h, j):
        span = pl.ds(j * CAP, CAP)
        return pltpu.make_async_remote_copy(
            fsend.at[t, h, span], fetched[t * HALVES + h].at[span],
            fs_sem.at[t, h, j - 1], fr_sem.at[t, h, j - 1],
            device_id=at_blk(-offset_of(j)), device_id_type=MESH,
        )

    def b_copy(t, h, j):
        span = pl.ds(j * CAP, CAP)
        return pltpu.make_async_remote_copy(
            bsend.at[t, h, span], brecv.at[t, h, span],
            bs_sem.at[t, h, j - 1], br_sem.at[t, h, j - 1],
            device_id=at_blk(offset_of(j)), device_id_type=MESH,
        )

    def f_fill(t, h):
        for n in range(SLOTS):
            block = state[trans_in[0, n], pl.ds(h * hs, hs)]
            if n < CAP:
                fetched[t * HALVES + h][n] = block
            else:
                fsend[t, h, n] = block

    def b_fill(t, h):
        where = pl.ds(t * sets + h * hs, hs)
        for i in range(tiles_dev):
            terms[i] = dot_nn(adj[row_in[i], where], tiles[i]).astype(BF16)
        for n in range(SLOTS):
            block = terms[tile_s[n]]
            if n < CAP:
                brecv[t, h, n] = block
            else:
                bsend[t, h, n] = block

    def f_step(t, h):
        total = [None] * blocks
        for i in range(tiles_dev):
            part = dot_nt(fetched[t * HALVES + h][slot_s[i]], tiles[i])
            for r in range(blocks):
                kept = part * rowmask[i * blocks + r]
                total[r] = kept if total[r] is None else total[r] + kept
        for r in range(blocks):
            state[r, pl.ds(h * hs, hs)] = total[r].astype(BF16)

    def b_step(t, h):
        total = [None] * blocks
        for n in range(SLOTS):
            part = brecv[t, h, n].astype(F32)
            for c in range(blocks):
                kept = part * transmask[n * blocks + c]
                total[c] = kept if total[c] is None else total[c] + kept
        return total

    loads[0].wait()
    ids = pores[...]
    low = lax.bitwise_and(ids, width - 1)
    unit = lax.shift_left(jnp.ones_like(ids), lax.shift_right_logical(ids, 7) * 8)
    lanes = lax.broadcasted_iota(jnp.int32, (sets, width), 1)
    counts = jnp.zeros((sets, width), jnp.int32)
    for e in range(ids.shape[1]):
        counts = counts + jnp.where(low[:, e : e + 1] == lanes, unit[:, e : e + 1], 0)
    for c in range(blocks):
        one = lax.bitwise_and(lax.shift_right_logical(counts, 8 * c), 255)
        state[c] = one.astype(F32).astype(BF16)
    for h in range(HALVES):
        f_fill(0, h)
    pl.semaphore_wait(barrier, NEIGH + n_inj - 1)
    for h in range(HALVES):
        for j in range(1, NEIGH + 1):
            f_copy(0, h, j).start()
    for load in loads[1:]:
        load.wait()
    for h in range(HALVES):
        b_fill(STEPS - 1, h)
        for j in range(1, NEIGH + 1):
            b_copy(STEPS - 1, h, j).start()

    def transpose_pair(p):
        for r in range(blocks):
            both = adj[r, pl.ds(p * 2 * sets, 2 * sets)]
            adj_t[r, :, pl.ds(p * 2 * sets, 2 * sets)] = both.T

    for k in range(STEPS):
        last = k == STEPS - 1
        for h in range(HALVES):
            for j in range(1, NEIGH + 1):
                f_copy(k, h, j).wait_recv()
            if not last:
                f_step(k, h)
                f_fill(k + 1, h)
                for j in range(1, NEIGH + 1):
                    f_copy(k + 1, h, j).start()
        if last:
            for i in range(tiles_dev):
                columns = jnp.concatenate(
                    [fetched[t * HALVES + h][slot_s[i]] for t in range(STEPS) for h in range(HALVES)], axis=0
                )
                full = dot_nn(adj_t[row_in[i]], columns) * (1.0 / sets)
                full = full.astype(BF16)
                for p in range(n_inj):
                    gsend[p, i] = full[p * portion : (p + 1) * portion]
            g_copies = []
            for o in range(1, n_inj):
                to = at_inj(o)
                g_copies.append(
                    pltpu.make_async_remote_copy(
                        gsend.at[to], grecv.at[o - 1], gs_sem.at[o - 1], gr_sem.at[o - 1],
                        device_id=(to, me_b), device_id_type=MESH,
                    )
                )
                g_copies[-1].start()
        back = STEPS - 1 - k
        for h in range(HALVES):
            for j in range(1, NEIGH + 1):
                b_copy(back, h, j).wait_recv()
            total = b_step(back, h)
            if last:
                for c in range(blocks):
                    sens_ref[pl.ds(h * hs, hs), pl.ds(c * width, width)] = total[c].astype(BF16)
            else:
                for c in range(blocks):
                    adj[c, pl.ds((back - 1) * sets + h * hs, hs)] = total[c].astype(BF16)
                b_fill(back - 1, h)
                for j in range(1, NEIGH + 1):
                    b_copy(back - 1, h, j).start()
        if k == 0:
            transpose_pair(1)
        if k == STEPS - 2:
            transpose_pair(0)
    for copy in g_copies:
        copy.wait_recv()
    mine = gsend[me_i].astype(F32)
    for o in range(1, n_inj):
        mine = mine + grecv[o - 1].astype(F32)
    grad_ref[...] = mine.astype(BF16)
    for copy in g_copies:
        copy.wait_send()
    for t in range(STEPS):
        for h in range(HALVES):
            for j in range(1, NEIGH + 1):
                f_copy(t, h, j).wait_send()
                b_copy(t, h, j).wait_send()


def shards(tile_values, tile_row, tile_dest, trans_block, inj_pores, final_weight):
    tiles_dev, width = tile_values.shape[:2]
    sets, pores = final_weight.shape
    blocks = pores // width
    n_inj, n_blk = lax.axis_size("inj"), lax.axis_size("blk")
    portion = width // n_inj
    hs = sets // HALVES
    smem = pl.BlockSpec(memory_space=pltpu.SMEM)
    hbm = pl.BlockSpec(memory_space=pl.ANY)
    vmem = pl.BlockSpec(memory_space=pltpu.VMEM)
    dma = pltpu.SemaphoreType.DMA
    return pl.pallas_call(
        functools.partial(sweep, n_inj, n_blk, blocks, tiles_dev),
        name="sweep",
        out_shape=(
            jax.ShapeDtypeStruct((sets, pores), BF16),
            jax.ShapeDtypeStruct((tiles_dev, portion, width), BF16),
        ),
        in_specs=[smem, smem, smem, hbm, hbm, hbm],
        out_specs=(vmem, vmem),
        scratch_shapes=[
            pltpu.VMEM((tiles_dev, width, width), BF16),
            pltpu.VMEM(inj_pores.shape, jnp.int32),
            pltpu.VMEM((blocks, sets, width), BF16),
            pltpu.VMEM((blocks, STEPS * sets, width), BF16),
            pltpu.VMEM((blocks, width, STEPS * sets), BF16),
            pltpu.VMEM((tiles_dev + 1, hs, width), BF16),
            pltpu.VMEM((STEPS, HALVES, SLOTS, hs, width), BF16),
            pltpu.VMEM((STEPS, HALVES, SLOTS, hs, width), BF16),
            pltpu.VMEM((STEPS, HALVES, SLOTS, hs, width), BF16),
            pltpu.VMEM((n_inj, tiles_dev, portion, width), BF16),
            pltpu.VMEM((n_inj - 1, tiles_dev, portion, width), BF16),
            pltpu.SMEM((tiles_dev,), jnp.int32),
            pltpu.SMEM((SLOTS,), jnp.int32),
            pltpu.SMEM((tiles_dev * blocks,), F32),
            pltpu.SMEM((SLOTS * blocks,), F32),
            dma((2 + blocks,)),
            dma((STEPS, HALVES, NEIGH)),
            dma((STEPS, HALVES, NEIGH)),
            dma((STEPS, HALVES, NEIGH)),
            dma((STEPS, HALVES, NEIGH)),
            dma((n_inj - 1,)),
            dma((n_inj - 1,)),
        ]
        + [pltpu.VMEM((SLOTS, hs, width), BF16)] * (STEPS * HALVES),
        compiler_params=pltpu.CompilerParams(
            collective_id=0, has_side_effects=True, vmem_limit_bytes=32 * 1024 * 1024
        ),
    )(tile_row, tile_dest, trans_block, tile_values, inj_pores, final_weight)


def solution(mesh):
    placed = (
        P("blk", None, None),
        P("blk"),
        P("blk", None),
        P("blk", None),
        P("inj", "blk"),
        P("inj", "blk"),
    )
    return jax.shard_map(
        shards,
        mesh=mesh,
        in_specs=placed,
        out_specs=(P("inj", "blk"), P("blk", "inj", None)),
        check_vma=False,
    )
```

```python
import functools

import jax
import jax.numpy as jnp
from jax import lax
from jax.experimental import pallas as pl
from jax.experimental.pallas import tpu as pltpu
from jax.sharding import PartitionSpec as P

NEIGH = 6
STEPS = 4
CAP = 3
SLOTS = (NEIGH + 1) * CAP
HF = 1
HB = 1
MESH = pl.DeviceIdType.MESH
F32 = jnp.float32
BF16 = jnp.bfloat16


def offset_of(slot):
    amount = (slot + 1) // 2
    return amount if slot % 2 == 1 else -amount


def dot_nt(x, y):
    return lax.dot_general(x, y, (((1,), (1,)), ((), ())), preferred_element_type=F32)


def dot_nn(x, y):
    return lax.dot_general(x, y, (((1,), (0,)), ((), ())), preferred_element_type=F32)


def sweep(
    n_inj, n_blk, blocks, tiles_dev, row_hbm, dest_hbm, trans_hbm, tiles_hbm, pores_hbm, weight_hbm,
    sens_hbm, parts_hbm, row_in, dest_in, trans_in, sens_ref, tiles, pores, state, adj, adj_t, terms, fsend, bsend, brecv, gsend,
    slot_s, tile_s, rowmask, transmask, in_sem, fs_sem, fr_sem, bs_sem, br_sem, gs_sem, gr_sem, *fetched,
):
    me_i, me_b = lax.axis_index("inj"), lax.axis_index("blk")
    sets = pores.shape[0]
    fs, bs = sets // HF, sets // HB
    width = tiles.shape[-1]
    portion = width // n_inj

    def at_blk(distance):
        return (me_i, lax.rem(me_b + (distance + n_blk), n_blk))

    def at_inj(distance):
        return lax.rem(me_i + distance, n_inj)

    small = [
        pltpu.make_async_copy(trans_hbm, trans_in, in_sem.at[4 + blocks]),
        pltpu.make_async_copy(row_hbm, row_in, in_sem.at[5 + blocks]),
        pltpu.make_async_copy(dest_hbm, dest_in, in_sem.at[6 + blocks]),
    ]
    loads = [
        pltpu.make_async_copy(pores_hbm, pores, in_sem.at[0]),
        pltpu.make_async_copy(tiles_hbm, tiles, in_sem.at[1]),
    ]
    for c in range(blocks):
        loads.append(
            pltpu.make_async_copy(
                weight_hbm.at[:, pl.ds(c * width, width)],
                adj.at[c, pl.ds((STEPS - 1) * sets, sets)],
                in_sem.at[2 + c],
            )
        )
    loads[0].start()
    for load in small + loads[1:]:
        load.start()

    barrier = pltpu.get_barrier_semaphore()
    for j in range(1, NEIGH + 1):
        pl.semaphore_signal(barrier, inc=1, device_id=at_blk(offset_of(j)), device_id_type=MESH)
    for o in range(1, n_inj):
        pl.semaphore_signal(barrier, inc=1, device_id=(at_inj(o), me_b), device_id_type=MESH)

    def f_copy(t, h, j):
        span = pl.ds(j * CAP, CAP)
        return pltpu.make_async_remote_copy(
            fsend.at[t, h, span], fetched[t * HF + h].at[span],
            fs_sem.at[t, h, j - 1], fr_sem.at[t, h, j - 1],
            device_id=at_blk(-offset_of(j)), device_id_type=MESH,
        )

    def b_copy(t, h, j):
        span = pl.ds(j * CAP, CAP)
        return pltpu.make_async_remote_copy(
            bsend.at[t, h, span], brecv.at[t, h, span],
            bs_sem.at[t, h, j - 1], br_sem.at[t, h, j - 1],
            device_id=at_blk(offset_of(j)), device_id_type=MESH,
        )

    def f_start(t, h):
        for j in range(1, NEIGH + 1):
            f_copy(t, h, j).start()

    def b_start(t, h):
        for j in range(1, NEIGH + 1):
            b_copy(t, h, j).start()

    def f_fill(t, h):
        for n in range(SLOTS):
            block = state[trans_in[0, n], pl.ds(h * fs, fs)]
            if n < CAP:
                fetched[t * HF + h][n] = block
            else:
                fsend[t, h, n] = block

    def b_fill(t, h):
        where = pl.ds(t * sets + h * bs, bs)
        for i in range(tiles_dev):
            terms[i] = dot_nn(adj[row_in[i], where], tiles[i]).astype(BF16)
        for n in range(SLOTS):
            block = terms[tile_s[n]]
            if n < CAP:
                brecv[t, h, n] = block
            else:
                bsend[t, h, n] = block

    def f_step(t, h):
        total = [None] * blocks
        for i in range(tiles_dev):
            part = dot_nt(fetched[t * HF + h][slot_s[i]], tiles[i])
            for r in range(blocks):
                kept = part * rowmask[i * blocks + r]
                total[r] = kept if total[r] is None else total[r] + kept
        for r in range(blocks):
            state[r, pl.ds(h * fs, fs)] = total[r].astype(BF16)

    def b_step(t, h):
        total = [None] * blocks
        for n in range(SLOTS):
            part = brecv[t, h, n].astype(F32)
            for c in range(blocks):
                kept = part * transmask[n * blocks + c]
                total[c] = kept if total[c] is None else total[c] + kept
        return total

    loads[0].wait()
    ids = pores[...]
    low = lax.bitwise_and(ids, width - 1)
    unit = lax.shift_left(jnp.ones_like(ids), lax.shift_right_logical(ids, 7) * 8)
    lanes = lax.broadcasted_iota(jnp.int32, (sets, width), 1)
    counts = jnp.zeros((sets, width), jnp.int32)
    for e in range(ids.shape[1]):
        counts = counts + jnp.where(low[:, e : e + 1] == lanes, unit[:, e : e + 1], 0)
    for c in range(blocks):
        one = lax.bitwise_and(lax.shift_right_logical(counts, 8 * c), 255)
        state[c] = one.astype(F32).astype(BF16)
    small[0].wait()
    for h in range(HF):
        f_fill(0, h)
    pl.semaphore_wait(barrier, NEIGH + n_inj - 1)
    for h in range(HF):
        f_start(0, h)
    small[1].wait()
    small[2].wait()

    dests = [dest_in[i] for i in range(tiles_dev)]
    slots = []
    for i in range(tiles_dev):
        earlier = jnp.int32(0)
        for e in range(i):
            earlier = earlier + jnp.where(dests[e] == dests[i], 1, 0)
        slots.append(dests[i] * CAP + earlier)
        slot_s[i] = slots[i]
    for n in range(SLOTS):
        user = jnp.int32(tiles_dev)
        for i in range(tiles_dev):
            user = jnp.where(slots[i] == n, i, user)
        tile_s[n] = user
    for i in range(tiles_dev):
        for r in range(blocks):
            rowmask[i * blocks + r] = jnp.where(row_in[i] == r, 1.0, 0.0).astype(F32)
    for n in range(SLOTS):
        for c in range(blocks):
            transmask[n * blocks + c] = jnp.where(trans_in[0, n] == c, 1.0, 0.0).astype(F32)
    terms[tiles_dev] = jnp.zeros_like(terms[tiles_dev])

    for load in loads[1:]:
        load.wait()
    for h in range(HB):
        b_fill(STEPS - 1, h)
    for h in range(HB):
        b_start(STEPS - 1, h)

    def transpose_pair(p):
        for r in range(blocks):
            both = adj[r, pl.ds(p * 2 * sets, 2 * sets)]
            adj_t[r, :, pl.ds(p * 2 * sets, 2 * sets)] = both.T

    for k in range(STEPS):
        last = k == STEPS - 1
        back = STEPS - 1 - k
        for h in range(HF):
            for j in range(1, NEIGH + 1):
                f_copy(k, h, j).wait_recv()
            if not last:
                f_step(k, h)
                f_fill(k + 1, h)
                f_start(k + 1, h)
        if last:
            for h in range(HB):
                b_start(0, h)
            for i in range(tiles_dev):
                columns = jnp.concatenate(
                    [fetched[t * HF + h][slot_s[i]] for t in range(STEPS) for h in range(HF)], axis=0
                )
                full = dot_nn(adj_t[row_in[i]], columns) * (1.0 / sets)
                full = full.astype(BF16)
                for p in range(n_inj):
                    gsend[p, i] = full[p * portion : (p + 1) * portion]
            own_out = pltpu.make_async_copy(gsend.at[me_i], parts_hbm.at[0], in_sem.at[3 + blocks])
            g_copies = []
            for o in range(1, n_inj):
                to = at_inj(o)
                g_copies.append(
                    pltpu.make_async_remote_copy(
                        gsend.at[to], parts_hbm.at[o], gs_sem.at[o - 1], gr_sem.at[o - 1],
                        device_id=(to, me_b), device_id_type=MESH,
                    )
                )
                g_copies[-1].start()
            own_out.start()
        for h in range(HB):
            for j in range(1, NEIGH + 1):
                b_copy(back, h, j).wait_recv()
            total = b_step(back, h)
            for c in range(blocks):
                if last:
                    sens_ref[pl.ds(h * bs, bs), pl.ds(c * width, width)] = total[c].astype(BF16)
                else:
                    adj[c, pl.ds((back - 1) * sets + h * bs, bs)] = total[c].astype(BF16)
            if not last:
                b_fill(back - 1, h)
                if back > 1:
                    b_start(back - 1, h)
        if k == 0:
            transpose_pair(1)
        if k == STEPS - 2:
            transpose_pair(0)
    sens_out = pltpu.make_async_copy(sens_ref, sens_hbm, in_sem.at[2 + blocks])
    sens_out.start()
    for copy in g_copies:
        copy.wait_recv()
    for copy in g_copies:
        copy.wait_send()
    for t in range(STEPS):
        for j in range(1, NEIGH + 1):
            for h in range(HF):
                f_copy(t, h, j).wait_send()
            for h in range(HB):
                b_copy(t, h, j).wait_send()
    sens_out.wait()
    own_out.wait()


def shards(tile_values, tile_row, tile_dest, trans_block, inj_pores, final_weight):
    tiles_dev, width = tile_values.shape[:2]
    sets, pores = final_weight.shape
    blocks = pores // width
    n_inj, n_blk = lax.axis_size("inj"), lax.axis_size("blk")
    portion = width // n_inj
    fs, bs = sets // HF, sets // HB
    hbm = pl.BlockSpec(memory_space=pl.ANY)
    dma = pltpu.SemaphoreType.DMA
    sensitivity, parts = pl.pallas_call(
        functools.partial(sweep, n_inj, n_blk, blocks, tiles_dev),
        name="sweep",
        out_shape=(
            jax.ShapeDtypeStruct((sets, pores), BF16),
            jax.ShapeDtypeStruct((n_inj, tiles_dev, portion, width), BF16),
        ),
        in_specs=[hbm] * 6,
        out_specs=(hbm, hbm),
        scratch_shapes=[
            pltpu.SMEM((tiles_dev,), jnp.int32),
            pltpu.SMEM((tiles_dev,), jnp.int32),
            pltpu.SMEM(trans_block.shape, jnp.int32),
            pltpu.VMEM((sets, pores), BF16),
            pltpu.VMEM((tiles_dev, width, width), BF16),
            pltpu.VMEM(inj_pores.shape, jnp.int32),
            pltpu.VMEM((blocks, sets, width), BF16),
            pltpu.VMEM((blocks, STEPS * sets, width), BF16),
            pltpu.VMEM((blocks, width, STEPS * sets), BF16),
            pltpu.VMEM((tiles_dev + 1, bs, width), BF16),
            pltpu.VMEM((STEPS, HF, SLOTS, fs, width), BF16),
            pltpu.VMEM((STEPS, HB, SLOTS, bs, width), BF16),
            pltpu.VMEM((STEPS, HB, SLOTS, bs, width), BF16),
            pltpu.VMEM((n_inj, tiles_dev, portion, width), BF16),
            pltpu.SMEM((tiles_dev,), jnp.int32),
            pltpu.SMEM((SLOTS,), jnp.int32),
            pltpu.SMEM((tiles_dev * blocks,), F32),
            pltpu.SMEM((SLOTS * blocks,), F32),
            dma((7 + blocks,)),
            dma((STEPS, HF, NEIGH)),
            dma((STEPS, HF, NEIGH)),
            dma((STEPS, HB, NEIGH)),
            dma((STEPS, HB, NEIGH)),
            dma((n_inj - 1,)),
            dma((n_inj - 1,)),
        ]
        + [pltpu.VMEM((SLOTS, fs, width), BF16)] * (STEPS * HF),
        compiler_params=pltpu.CompilerParams(
            collective_id=0, has_side_effects=True, vmem_limit_bytes=60 * 1024 * 1024
        ),
    )(tile_row, tile_dest[:, 0], trans_block, tile_values, inj_pores, final_weight)
    total = parts[0].astype(F32)
    for o in range(1, n_inj):
        total = total + parts[o].astype(F32)
    return sensitivity, total.astype(BF16)


def solution(mesh):
    placed = (
        P("blk", None, None),
        P("blk"),
        P("blk", None),
        P("blk", None),
        P("inj", "blk"),
        P("inj", "blk"),
    )
    return jax.shard_map(
        shards,
        mesh=mesh,
        in_specs=placed,
        out_specs=(P("inj", "blk"), P("blk", "inj", None)),
        check_vma=False,
    )
```

```python
import functools

import jax
import jax.numpy as jnp
from jax import lax
from jax.experimental import pallas as pl
from jax.experimental.pallas import tpu as pltpu
from jax.sharding import PartitionSpec as P

NEIGH = 6
STEPS = 4
CAP = 3
SLOTS = (NEIGH + 1) * CAP
HF = 2
HB = 2
MESH = pl.DeviceIdType.MESH
F32 = jnp.float32
BF16 = jnp.bfloat16


def offset_of(slot):
    amount = (slot + 1) // 2
    return amount if slot % 2 == 1 else -amount


def dot_nt(x, y):
    return lax.dot_general(x, y, (((1,), (1,)), ((), ())), preferred_element_type=F32)


def dot_nn(x, y):
    return lax.dot_general(x, y, (((1,), (0,)), ((), ())), preferred_element_type=F32)


def sweep(
    n_inj, n_blk, blocks, tiles_dev, row_hbm, dest_hbm, trans_hbm, tiles_hbm, pores_hbm, weight_hbm,
    sens_ref, grad_ref, row_in, dest_in, trans_in, tiles, pores, state, adj, adj_t, terms, fsend, bsend, brecv, gsend, grecv,
    slot_s, tile_s, rowmask, transmask, in_sem, fs_sem, fr_sem, bs_sem, br_sem, gs_sem, gr_sem, *fetched,
):
    me_i, me_b = lax.axis_index("inj"), lax.axis_index("blk")
    sets = pores.shape[0]
    fs, bs = sets // HF, sets // HB
    width = tiles.shape[-1]
    portion = width // n_inj

    def at_blk(distance):
        return (me_i, lax.rem(me_b + (distance + n_blk), n_blk))

    def at_inj(distance):
        return lax.rem(me_i + distance, n_inj)

    small = [
        pltpu.make_async_copy(trans_hbm, trans_in, in_sem.at[2 + blocks]),
        pltpu.make_async_copy(row_hbm, row_in, in_sem.at[3 + blocks]),
        pltpu.make_async_copy(dest_hbm, dest_in, in_sem.at[4 + blocks]),
    ]
    loads = [
        pltpu.make_async_copy(pores_hbm, pores, in_sem.at[0]),
        pltpu.make_async_copy(tiles_hbm, tiles, in_sem.at[1]),
    ]
    for c in range(blocks):
        loads.append(
            pltpu.make_async_copy(
                weight_hbm.at[:, pl.ds(c * width, width)],
                adj.at[c, pl.ds((STEPS - 1) * sets, sets)],
                in_sem.at[2 + c],
            )
        )
    loads[0].start()
    for load in small + loads[1:]:
        load.start()

    barrier = pltpu.get_barrier_semaphore()
    for j in range(1, NEIGH + 1):
        pl.semaphore_signal(barrier, inc=1, device_id=at_blk(offset_of(j)), device_id_type=MESH)
    for o in range(1, n_inj):
        pl.semaphore_signal(barrier, inc=1, device_id=(at_inj(o), me_b), device_id_type=MESH)

    def f_copy(t, h, j, count=1):
        span = pl.ds(j * CAP, count * CAP)
        return pltpu.make_async_remote_copy(
            fsend.at[t, h, span], fetched[t * HF + h].at[span],
            fs_sem.at[t, h], fr_sem.at[t, h],
            device_id=at_blk(-offset_of(j)), device_id_type=MESH,
        )

    def b_copy(t, h, j, count=1):
        span = pl.ds(j * CAP, count * CAP)
        return pltpu.make_async_remote_copy(
            bsend.at[t, h, span], brecv.at[t, h, span],
            bs_sem.at[t, h], br_sem.at[t, h],
            device_id=at_blk(offset_of(j)), device_id_type=MESH,
        )

    def f_start(t, h):
        for j in range(1, NEIGH + 1):
            f_copy(t, h, j).start()

    def f_all(t, h):
        return f_copy(t, h, 1, NEIGH)

    def b_start(t, h):
        for j in range(1, NEIGH + 1):
            b_copy(t, h, j).start()

    def b_all(t, h):
        return b_copy(t, h, 1, NEIGH)

    def f_fill(t, h):
        for n in range(SLOTS):
            block = state[trans_in[0, n], pl.ds(h * fs, fs)]
            if n < CAP:
                fetched[t * HF + h][n] = block
            else:
                fsend[t, h, n] = block

    def b_fill(t, h):
        where = pl.ds(t * sets + h * bs, bs)
        for i in range(tiles_dev):
            terms[i] = dot_nn(adj[row_in[i], where], tiles[i]).astype(BF16)
        for n in range(SLOTS):
            block = terms[tile_s[n]]
            if n < CAP:
                brecv[t, h, n] = block
            else:
                bsend[t, h, n] = block

    def f_step(t, h):
        total = [None] * blocks
        for i in range(tiles_dev):
            part = dot_nt(fetched[t * HF + h][slot_s[i]], tiles[i])
            for r in range(blocks):
                kept = part * rowmask[i * blocks + r]
                total[r] = kept if total[r] is None else total[r] + kept
        for r in range(blocks):
            state[r, pl.ds(h * fs, fs)] = total[r].astype(BF16)

    def b_step(t, h):
        total = [None] * blocks
        for n in range(SLOTS):
            part = brecv[t, h, n].astype(F32)
            for c in range(blocks):
                kept = part * transmask[n * blocks + c]
                total[c] = kept if total[c] is None else total[c] + kept
        return total

    loads[0].wait()
    ids = pores[...]
    low = lax.bitwise_and(ids, width - 1)
    unit = lax.shift_left(jnp.ones_like(ids), lax.shift_right_logical(ids, 7) * 8)
    lanes = lax.broadcasted_iota(jnp.int32, (sets, width), 1)
    counts = jnp.zeros((sets, width), jnp.int32)
    for e in range(ids.shape[1]):
        counts = counts + jnp.where(low[:, e : e + 1] == lanes, unit[:, e : e + 1], 0)
    for c in range(blocks):
        one = lax.bitwise_and(lax.shift_right_logical(counts, 8 * c), 255)
        state[c] = one.astype(F32).astype(BF16)
    small[0].wait()
    for h in range(HF):
        f_fill(0, h)
    pl.semaphore_wait(barrier, NEIGH + n_inj - 1)
    for h in range(HF):
        f_start(0, h)
    small[1].wait()
    small[2].wait()

    dests = [dest_in[i] for i in range(tiles_dev)]
    slots = []
    for i in range(tiles_dev):
        earlier = jnp.int32(0)
        for e in range(i):
            earlier = earlier + jnp.where(dests[e] == dests[i], 1, 0)
        slots.append(dests[i] * CAP + earlier)
        slot_s[i] = slots[i]
    for n in range(SLOTS):
        user = jnp.int32(tiles_dev)
        for i in range(tiles_dev):
            user = jnp.where(slots[i] == n, i, user)
        tile_s[n] = user
    for i in range(tiles_dev):
        for r in range(blocks):
            rowmask[i * blocks + r] = jnp.where(row_in[i] == r, 1.0, 0.0).astype(F32)
    for n in range(SLOTS):
        for c in range(blocks):
            transmask[n * blocks + c] = jnp.where(trans_in[0, n] == c, 1.0, 0.0).astype(F32)
    terms[tiles_dev] = jnp.zeros_like(terms[tiles_dev])

    for load in loads[1:]:
        load.wait()
    for h in range(HB):
        b_fill(STEPS - 1, h)
    for h in range(HB):
        b_start(STEPS - 1, h)

    def transpose_pair(p):
        for r in range(blocks):
            both = adj[r, pl.ds(p * 2 * sets, 2 * sets)]
            adj_t[r, :, pl.ds(p * 2 * sets, 2 * sets)] = both.T

    for k in range(STEPS):
        last = k == STEPS - 1
        back = STEPS - 1 - k
        for h in range(HF):
            if k:
                f_all(k - 1, h).wait_send()
            f_all(k, h).wait_recv()
            if not last:
                f_step(k, h)
                f_fill(k + 1, h)
                f_start(k + 1, h)
        if last:
            for h in range(HB):
                b_start(0, h)
            for i in range(tiles_dev):
                columns = jnp.concatenate(
                    [fetched[t * HF + h][slot_s[i]] for t in range(STEPS) for h in range(HF)], axis=0
                )
                full = dot_nn(adj_t[row_in[i]], columns) * (1.0 / sets)
                full = full.astype(BF16)
                for p in range(n_inj):
                    gsend[p, i] = full[p * portion : (p + 1) * portion]
            g_copies = []
            for o in range(1, n_inj):
                to = at_inj(o)
                g_copies.append(
                    pltpu.make_async_remote_copy(
                        gsend.at[to], grecv.at[o - 1], gs_sem.at[o - 1], gr_sem.at[o - 1],
                        device_id=(to, me_b), device_id_type=MESH,
                    )
                )
                g_copies[-1].start()
        for h in range(HB):
            if k:
                b_all(back + 1, h).wait_send()
            b_all(back, h).wait_recv()
            total = b_step(back, h)
            for c in range(blocks):
                if last:
                    sens_ref[pl.ds(h * bs, bs), pl.ds(c * width, width)] = total[c].astype(BF16)
                else:
                    adj[c, pl.ds((back - 1) * sets + h * bs, bs)] = total[c].astype(BF16)
            if not last:
                b_fill(back - 1, h)
                if back > 1:
                    b_start(back - 1, h)
        if k == 0:
            transpose_pair(1)
        if k == STEPS - 2:
            transpose_pair(0)
    for h in range(HF):
        f_all(STEPS - 1, h).wait_send()
    for h in range(HB):
        b_all(0, h).wait_send()
    for copy in g_copies:
        copy.wait_recv()
    mine = gsend[me_i].astype(F32)
    for o in range(1, n_inj):
        mine = mine + grecv[o - 1].astype(F32)
    grad_ref[...] = mine.astype(BF16)
    for copy in g_copies:
        copy.wait_send()


def shards(tile_values, tile_row, tile_dest, trans_block, inj_pores, final_weight):
    tiles_dev, width = tile_values.shape[:2]
    sets, pores = final_weight.shape
    blocks = pores // width
    n_inj, n_blk = lax.axis_size("inj"), lax.axis_size("blk")
    portion = width // n_inj
    fs, bs = sets // HF, sets // HB
    vmem = pl.BlockSpec(memory_space=pltpu.VMEM)
    hbm = pl.BlockSpec(memory_space=pl.ANY)
    dma = pltpu.SemaphoreType.DMA
    return pl.pallas_call(
        functools.partial(sweep, n_inj, n_blk, blocks, tiles_dev),
        name="sweep",
        out_shape=(pltpu.VMEM((sets, pores), BF16), pltpu.VMEM((tiles_dev, portion, width), BF16)),
        in_specs=[hbm] * 6,
        out_specs=(vmem, vmem),
        scratch_shapes=[
            pltpu.SMEM((tiles_dev,), jnp.int32),
            pltpu.SMEM((tiles_dev,), jnp.int32),
            pltpu.SMEM(trans_block.shape, jnp.int32),
            pltpu.VMEM((tiles_dev, width, width), BF16),
            pltpu.VMEM(inj_pores.shape, jnp.int32),
            pltpu.VMEM((blocks, sets, width), BF16),
            pltpu.VMEM((blocks, STEPS * sets, width), BF16),
            pltpu.VMEM((blocks, width, STEPS * sets), BF16),
            pltpu.VMEM((tiles_dev + 1, bs, width), BF16),
            pltpu.VMEM((STEPS, HF, SLOTS, fs, width), BF16),
            pltpu.VMEM((STEPS, HB, SLOTS, bs, width), BF16),
            pltpu.VMEM((STEPS, HB, SLOTS, bs, width), BF16),
            pltpu.VMEM((n_inj, tiles_dev, portion, width), BF16),
            pltpu.VMEM((n_inj - 1, tiles_dev, portion, width), BF16),
            pltpu.SMEM((tiles_dev,), jnp.int32),
            pltpu.SMEM((SLOTS,), jnp.int32),
            pltpu.SMEM((tiles_dev * blocks,), F32),
            pltpu.SMEM((SLOTS * blocks,), F32),
            dma((5 + blocks,)),
            dma((STEPS, HF)),
            dma((STEPS, HF)),
            dma((STEPS, HB)),
            dma((STEPS, HB)),
            dma((n_inj - 1,)),
            dma((n_inj - 1,)),
        ]
        + [pltpu.VMEM((SLOTS, fs, width), BF16)] * (STEPS * HF),
        compiler_params=pltpu.CompilerParams(
            collective_id=0, has_side_effects=True, vmem_limit_bytes=60 * 1024 * 1024
        ),
    )(tile_row, tile_dest[:, 0], trans_block, tile_values, inj_pores, final_weight)


def solution(mesh):
    placed = (
        P("blk", None, None),
        P("blk"),
        P("blk", None),
        P("blk", None),
        P("inj", "blk"),
        P("inj", "blk"),
    )
    return jax.shard_map(
        shards,
        mesh=mesh,
        in_specs=placed,
        out_specs=(P("inj", "blk"), P("blk", "inj", None)),
        check_vma=False,
    )
```

```python
import functools

import jax
import jax.numpy as jnp
from jax import lax
from jax.experimental import pallas as pl
from jax.experimental.pallas import tpu as pltpu
from jax.sharding import PartitionSpec as P

NEIGH = 6
STEPS = 4
CAP = 3
SLOTS = (NEIGH + 1) * CAP
HF = 2
HB = 2
MESH = pl.DeviceIdType.MESH
F32 = jnp.float32
BF16 = jnp.bfloat16


def offset_of(slot):
    amount = (slot + 1) // 2
    return amount if slot % 2 == 1 else -amount


def dot_nt(x, y):
    return lax.dot_general(x, y, (((1,), (1,)), ((), ())), preferred_element_type=F32)


def dot_nn(x, y):
    return lax.dot_general(x, y, (((1,), (0,)), ((), ())), preferred_element_type=F32)


def sweep(
    n_inj, n_blk, blocks, tiles_dev, row_hbm, dest_hbm, trans_hbm, tiles_hbm, pores_hbm, weight_hbm,
    sens_ref, grad_ref, row_in, dest_in, trans_in, tiles, pores, state, adj, adj_t, terms, fsend, bsend, brecv, gsend, grecv,
    gsum, slot_s, tile_s, perm_s, place_s, rowmask, transmask, in_sem, fs_sem, fr_sem, bs_sem, br_sem, gs_sem, gr_sem, *fetched,
):
    me_i, me_b = lax.axis_index("inj"), lax.axis_index("blk")
    sets = pores.shape[0]
    fs, bs = sets // HF, sets // HB
    width = tiles.shape[-1]
    portion = width // n_inj

    def at_blk(distance):
        return (me_i, lax.rem(me_b + (distance + n_blk), n_blk))

    def at_inj(distance):
        return lax.rem(me_i + distance, n_inj)

    first = pltpu.make_async_copy(pores_hbm, pores, in_sem.at[0])
    first.start()
    barrier = pltpu.get_barrier_semaphore()
    for j in range(NEIGH, 0, -1):
        pl.semaphore_signal(barrier, inc=1, device_id=at_blk(offset_of(j)), device_id_type=MESH)
    for o in range(1, n_inj):
        pl.semaphore_signal(barrier, inc=1, device_id=(at_inj(o), me_b), device_id_type=MESH)

    small = [
        pltpu.make_async_copy(trans_hbm, trans_in, in_sem.at[2 + blocks]),
        pltpu.make_async_copy(row_hbm, row_in, in_sem.at[3 + blocks]),
        pltpu.make_async_copy(dest_hbm, dest_in, in_sem.at[4 + blocks]),
    ]
    loads = [
        pltpu.make_async_copy(tiles_hbm, tiles, in_sem.at[1]),
    ]
    for c in range(blocks):
        loads.append(
            pltpu.make_async_copy(
                weight_hbm.at[:, pl.ds(c * width, width)],
                adj.at[c, pl.ds((STEPS - 1) * sets, sets)],
                in_sem.at[2 + c],
            )
        )
    for load in small + loads:
        load.start()

    def f_copy(t, h, j, count=1):
        span = pl.ds(j * CAP, count * CAP)
        return pltpu.make_async_remote_copy(
            fsend.at[t, h, span], fetched[t * HF + h].at[span],
            fs_sem.at[t, h], fr_sem.at[t, h],
            device_id=at_blk(-offset_of(j)), device_id_type=MESH,
        )

    def b_copy(t, h, j, count=1):
        span = pl.ds(j * CAP, count * CAP)
        return pltpu.make_async_remote_copy(
            bsend.at[t, h, span], brecv.at[t, h, span],
            bs_sem.at[t, h], br_sem.at[t, h],
            device_id=at_blk(offset_of(j)), device_id_type=MESH,
        )

    def f_start(t, h):
        for j in range(1, NEIGH + 1):
            f_copy(t, h, j).start()

    def f_all(t, h):
        return f_copy(t, h, 1, NEIGH)

    def b_start(t, h):
        for j in range(1, NEIGH + 1):
            b_copy(t, h, j).start()

    def b_all(t, h):
        return b_copy(t, h, 1, NEIGH)

    def f_fill(t, h):
        for n in range(SLOTS):
            block = state[trans_in[0, n], pl.ds(h * fs, fs)]
            if n < CAP:
                fetched[t * HF + h][n] = block
            else:
                fsend[t, h, n] = block

    def b_fill(t, h):
        where = pl.ds(t * sets + h * bs, bs)
        for i in range(tiles_dev):
            terms[i] = dot_nn(adj[row_in[i], where], tiles[i]).astype(BF16)
        for n in range(SLOTS):
            block = terms[tile_s[n]]
            if n < CAP:
                brecv[t, h, n] = block
            else:
                bsend[t, h, n] = block

    def f_step(t, h):
        total = [None] * blocks
        for i in range(tiles_dev):
            part = dot_nt(fetched[t * HF + h][slot_s[i]], tiles[i])
            for r in range(blocks):
                kept = part * rowmask[i * blocks + r]
                total[r] = kept if total[r] is None else total[r] + kept
        for r in range(blocks):
            state[r, pl.ds(h * fs, fs)] = total[r].astype(BF16)

    def b_step(t, h):
        total = [None] * blocks
        for n in range(SLOTS):
            part = brecv[t, h, n].astype(F32)
            for c in range(blocks):
                kept = part * transmask[n * blocks + c]
                total[c] = kept if total[c] is None else total[c] + kept
        return total

    first.wait()
    ids = pores[...]
    low = lax.bitwise_and(ids, width - 1)
    unit = lax.shift_left(jnp.ones_like(ids), lax.shift_right_logical(ids, 7) * 8)
    lanes = lax.broadcasted_iota(jnp.int32, (sets, width), 1)
    counts = jnp.zeros((sets, width), jnp.int32)
    for e in range(ids.shape[1]):
        counts = counts + jnp.where(low[:, e : e + 1] == lanes, unit[:, e : e + 1], 0)
    for c in range(blocks):
        one = lax.bitwise_and(lax.shift_right_logical(counts, 8 * c), 255)
        state[c] = one.astype(F32).astype(BF16)
    small[0].wait()
    for h in range(HF):
        f_fill(0, h)
    pl.semaphore_wait(barrier, NEIGH + n_inj - 1)
    for h in range(HF):
        f_start(0, h)
    small[1].wait()
    small[2].wait()

    dests = [dest_in[i] for i in range(tiles_dev)]
    slots = []
    for i in range(tiles_dev):
        earlier = jnp.int32(0)
        for e in range(i):
            earlier = earlier + jnp.where(dests[e] == dests[i], 1, 0)
        slots.append(dests[i] * CAP + earlier)
        slot_s[i] = slots[i]
    for n in range(SLOTS):
        user = jnp.int32(tiles_dev)
        for i in range(tiles_dev):
            user = jnp.where(slots[i] == n, i, user)
        tile_s[n] = user
    before, ranks = jnp.int32(0), []
    for i in range(tiles_dev):
        own = dests[i] == 0
        ranks.append(jnp.where(own, slots[i], CAP + i - before))
        before = before + jnp.where(own, 1, 0)
        place_s[i] = ranks[i]
    for q in range(tiles_dev):
        user = jnp.int32(0)
        for i in range(tiles_dev):
            user = jnp.where(ranks[i] == q, i, user)
        perm_s[q] = user
    for i in range(tiles_dev):
        for r in range(blocks):
            rowmask[i * blocks + r] = jnp.where(row_in[i] == r, 1.0, 0.0).astype(F32)
    for n in range(SLOTS):
        for c in range(blocks):
            transmask[n * blocks + c] = jnp.where(trans_in[0, n] == c, 1.0, 0.0).astype(F32)
    terms[tiles_dev] = jnp.zeros_like(terms[tiles_dev])

    for load in loads:
        load.wait()
    for h in range(HB):
        b_fill(STEPS - 1, h)
    for h in range(HB):
        b_start(STEPS - 1, h)

    def g_copy(part, o):
        to = at_inj(o)
        span = pl.ds(CAP, tiles_dev - CAP) if part else pl.ds(0, CAP)
        return pltpu.make_async_remote_copy(
            gsend.at[to, span], grecv.at[o - 1, span], gs_sem.at[part, o - 1], gr_sem.at[part, o - 1],
            device_id=(to, me_b), device_id_type=MESH,
        )

    def gradient(part):
        for q in range(CAP, tiles_dev) if part else range(CAP):
            i = perm_s[q]
            slot = slot_s[i] if part else q
            columns = jnp.concatenate([fetched[t * HF + h][slot] for t in range(STEPS) for h in range(HF)], axis=0)
            full = dot_nn(adj_t[row_in[i]], columns) * (1.0 / sets)
            full = full.astype(BF16)
            for p in range(n_inj):
                gsend[p, q] = full[p * portion : (p + 1) * portion]
        for o in range(1, n_inj):
            g_copy(part, o).start()

    def g_sum(part):
        for o in range(1, n_inj):
            g_copy(part, o).wait_send()
            g_copy(part, o).wait_recv()
        span = pl.ds(CAP, tiles_dev - CAP) if part else pl.ds(0, CAP)
        mine = gsend[me_i, span].astype(F32)
        for o in range(1, n_inj):
            mine = mine + grecv[o - 1, span].astype(F32)
        gsum[span] = mine.astype(BF16)

    def transpose_pair(p):
        for r in range(blocks):
            both = adj[r, pl.ds(p * 2 * sets, 2 * sets)]
            adj_t[r, :, pl.ds(p * 2 * sets, 2 * sets)] = both.T

    for k in range(STEPS):
        last = k == STEPS - 1
        back = STEPS - 1 - k
        for h in range(HF):
            if k:
                f_all(k - 1, h).wait_send()
            f_all(k, h).wait_recv()
            if not last:
                f_step(k, h)
                f_fill(k + 1, h)
                f_start(k + 1, h)
        if last:
            for h in range(HB):
                b_start(0, h)
            gradient(1)
        for h in range(HB):
            if k:
                b_all(back + 1, h).wait_send()
            b_all(back, h).wait_recv()
            total = b_step(back, h)
            for c in range(blocks):
                if last:
                    sens_ref[pl.ds(h * bs, bs), pl.ds(c * width, width)] = total[c].astype(BF16)
                else:
                    adj[c, pl.ds((back - 1) * sets + h * bs, bs)] = total[c].astype(BF16)
            if not last:
                b_fill(back - 1, h)
                if back > 1:
                    b_start(back - 1, h)
        if k == 0:
            transpose_pair(1)
        if k == STEPS - 2:
            transpose_pair(0)
            gradient(0)
    for h in range(HF):
        f_all(STEPS - 1, h).wait_send()
    for h in range(HB):
        b_all(0, h).wait_send()
    for part in range(2):
        g_sum(part)
    for i in range(tiles_dev):
        grad_ref[i] = gsum[place_s[i]]


def shards(tile_values, tile_row, tile_dest, trans_block, inj_pores, final_weight):
    tiles_dev, width = tile_values.shape[:2]
    sets, pores = final_weight.shape
    blocks = pores // width
    n_inj, n_blk = lax.axis_size("inj"), lax.axis_size("blk")
    portion = width // n_inj
    fs, bs = sets // HF, sets // HB
    vmem = pl.BlockSpec(memory_space=pltpu.VMEM)
    hbm = pl.BlockSpec(memory_space=pl.ANY)
    dma = pltpu.SemaphoreType.DMA
    return pl.pallas_call(
        functools.partial(sweep, n_inj, n_blk, blocks, tiles_dev),
        name="sweep",
        out_shape=(pltpu.VMEM((sets, pores), BF16), pltpu.VMEM((tiles_dev, portion, width), BF16)),
        in_specs=[hbm] * 6,
        out_specs=(vmem, vmem),
        scratch_shapes=[
            pltpu.SMEM((tiles_dev,), jnp.int32),
            pltpu.SMEM((tiles_dev,), jnp.int32),
            pltpu.SMEM(trans_block.shape, jnp.int32),
            pltpu.VMEM((tiles_dev, width, width), BF16),
            pltpu.VMEM(inj_pores.shape, jnp.int32),
            pltpu.VMEM((blocks, sets, width), BF16),
            pltpu.VMEM((blocks, STEPS * sets, width), BF16),
            pltpu.VMEM((blocks, width, STEPS * sets), BF16),
            pltpu.VMEM((tiles_dev + 1, bs, width), BF16),
            pltpu.VMEM((STEPS, HF, SLOTS, fs, width), BF16),
            pltpu.VMEM((STEPS, HB, SLOTS, bs, width), BF16),
            pltpu.VMEM((STEPS, HB, SLOTS, bs, width), BF16),
            pltpu.VMEM((n_inj, tiles_dev, portion, width), BF16),
            pltpu.VMEM((n_inj - 1, tiles_dev, portion, width), BF16),
            pltpu.VMEM((tiles_dev, portion, width), BF16),
            pltpu.SMEM((tiles_dev,), jnp.int32),
            pltpu.SMEM((SLOTS,), jnp.int32),
            pltpu.SMEM((tiles_dev,), jnp.int32),
            pltpu.SMEM((tiles_dev,), jnp.int32),
            pltpu.SMEM((tiles_dev * blocks,), F32),
            pltpu.SMEM((SLOTS * blocks,), F32),
            dma((5 + blocks,)),
            dma((STEPS, HF)),
            dma((STEPS, HF)),
            dma((STEPS, HB)),
            dma((STEPS, HB)),
            dma((2, n_inj - 1)),
            dma((2, n_inj - 1)),
        ]
        + [pltpu.VMEM((SLOTS, fs, width), BF16)] * (STEPS * HF),
        compiler_params=pltpu.CompilerParams(
            collective_id=0, has_side_effects=True, vmem_limit_bytes=60 * 1024 * 1024
        ),
    )(tile_row, tile_dest[:, 0], trans_block, tile_values, inj_pores, final_weight)


def solution(mesh):
    placed = (
        P("blk", None, None),
        P("blk"),
        P("blk", None),
        P("blk", None),
        P("inj", "blk"),
        P("inj", "blk"),
    )
    return jax.shard_map(
        shards,
        mesh=mesh,
        in_specs=placed,
        out_specs=(P("inj", "blk"), P("blk", "inj", None)),
        check_vma=False,
    )
```

```python
import functools

import jax
import jax.numpy as jnp
from jax import lax
from jax.experimental import pallas as pl
from jax.experimental.pallas import tpu as pltpu
from jax.sharding import PartitionSpec as P

NEIGH = 6
STEPS = 4
CAP = 3
SLOTS = (NEIGH + 1) * CAP
ORDER = (3, 4, 5, 6, 1, 2)
HF = 2
HB = 2
MESH = pl.DeviceIdType.MESH
F32 = jnp.float32
BF16 = jnp.bfloat16


def offset_of(slot):
    amount = (slot + 1) // 2
    return amount if slot % 2 == 1 else -amount


def dot_nt(x, y):
    return lax.dot_general(x, y, (((1,), (1,)), ((), ())), preferred_element_type=F32)


def dot_nn(x, y):
    return lax.dot_general(x, y, (((1,), (0,)), ((), ())), preferred_element_type=F32)


def sweep(
    n_inj, n_blk, blocks, tiles_dev, row_hbm, dest_hbm, trans_hbm, tiles_hbm, pores_hbm, weight_hbm,
    sens_ref, grad_ref, row_in, dest_in, trans_in, tiles, pores, state, adj, adj_t, terms, fsend, bsend, brecv, gsend, grecv,
    gsum, slot_s, tile_s, perm_s, place_s, rowmask, transmask, in_sem, fs_sem, fr_sem, bs_sem, br_sem, gs_sem, gr_sem, *fetched,
):
    me_i, me_b = lax.axis_index("inj"), lax.axis_index("blk")
    sets = pores.shape[0]
    fs, bs = sets // HF, sets // HB
    width = tiles.shape[-1]
    portion = width // n_inj

    def at_blk(distance):
        return (me_i, lax.rem(me_b + (distance + n_blk), n_blk))

    def at_inj(distance):
        return lax.rem(me_i + distance, n_inj)

    first = pltpu.make_async_copy(pores_hbm, pores, in_sem.at[0])
    first.start()
    barrier = pltpu.get_barrier_semaphore()
    for j in range(NEIGH, 0, -1):
        pl.semaphore_signal(barrier, inc=1, device_id=at_blk(offset_of(j)), device_id_type=MESH)
    for o in range(1, n_inj):
        pl.semaphore_signal(barrier, inc=1, device_id=(at_inj(o), me_b), device_id_type=MESH)

    small = [
        pltpu.make_async_copy(trans_hbm, trans_in, in_sem.at[2 + blocks]),
        pltpu.make_async_copy(row_hbm, row_in, in_sem.at[3 + blocks]),
        pltpu.make_async_copy(dest_hbm, dest_in, in_sem.at[4 + blocks]),
    ]
    loads = [
        pltpu.make_async_copy(tiles_hbm, tiles, in_sem.at[1]),
    ]
    for c in range(blocks):
        loads.append(
            pltpu.make_async_copy(
                weight_hbm.at[:, pl.ds(c * width, width)],
                adj.at[c, pl.ds((STEPS - 1) * sets, sets)],
                in_sem.at[2 + c],
            )
        )
    for load in small + loads:
        load.start()

    def f_copy(t, h, j, count=1):
        span = pl.ds(j * CAP, count * CAP)
        return pltpu.make_async_remote_copy(
            fsend.at[t, h, span], fetched[t * HF + h].at[span],
            fs_sem.at[t, h], fr_sem.at[t, h],
            device_id=at_blk(-offset_of(j)), device_id_type=MESH,
        )

    def b_copy(t, h, j, count=1):
        span = pl.ds(j * CAP, count * CAP)
        return pltpu.make_async_remote_copy(
            bsend.at[t, h, span], brecv.at[t, h, span],
            bs_sem.at[t, h], br_sem.at[t, h],
            device_id=at_blk(offset_of(j)), device_id_type=MESH,
        )

    def f_start(t, h):
        for j in ORDER:
            f_copy(t, h, j).start()

    def f_all(t, h):
        return f_copy(t, h, 1, NEIGH)

    def b_start(t, h):
        for j in ORDER:
            b_copy(t, h, j).start()

    def b_all(t, h):
        return b_copy(t, h, 1, NEIGH)

    def f_fill(t, h):
        for n in range(SLOTS):
            block = state[trans_in[0, n], pl.ds(h * fs, fs)]
            if n < CAP:
                fetched[t * HF + h][n] = block
            else:
                fsend[t, h, n] = block

    def b_fill(t, h):
        where = pl.ds(t * sets + h * bs, bs)
        for i in range(tiles_dev):
            terms[i] = dot_nn(adj[row_in[i], where], tiles[i]).astype(BF16)
        for n in range(SLOTS):
            block = terms[tile_s[n]]
            if n < CAP:
                brecv[t, h, n] = block
            else:
                bsend[t, h, n] = block

    def f_step(t, h):
        total = [None] * blocks
        for i in range(tiles_dev):
            part = dot_nt(fetched[t * HF + h][slot_s[i]], tiles[i])
            for r in range(blocks):
                kept = part * rowmask[i * blocks + r]
                total[r] = kept if total[r] is None else total[r] + kept
        for r in range(blocks):
            state[r, pl.ds(h * fs, fs)] = total[r].astype(BF16)

    def b_step(t, h):
        total = [None] * blocks
        for n in range(SLOTS):
            part = brecv[t, h, n].astype(F32)
            for c in range(blocks):
                kept = part * transmask[n * blocks + c]
                total[c] = kept if total[c] is None else total[c] + kept
        return total

    first.wait()
    ids = pores[...]
    low = lax.bitwise_and(ids, width - 1)
    unit = lax.shift_left(jnp.ones_like(ids), lax.shift_right_logical(ids, 7) * 8)
    lanes = lax.broadcasted_iota(jnp.int32, (sets, width), 1)
    counts = jnp.zeros((sets, width), jnp.int32)
    for e in range(ids.shape[1]):
        counts = counts + jnp.where(low[:, e : e + 1] == lanes, unit[:, e : e + 1], 0)
    for c in range(blocks):
        one = lax.bitwise_and(lax.shift_right_logical(counts, 8 * c), 255)
        state[c] = one.astype(F32).astype(BF16)
    small[0].wait()
    for h in range(HF):
        f_fill(0, h)
    pl.semaphore_wait(barrier, NEIGH + n_inj - 1)
    for h in range(HF):
        f_start(0, h)
    small[1].wait()
    small[2].wait()

    dests = [dest_in[i] for i in range(tiles_dev)]
    slots = []
    for i in range(tiles_dev):
        earlier = jnp.int32(0)
        for e in range(i):
            earlier = earlier + jnp.where(dests[e] == dests[i], 1, 0)
        slots.append(dests[i] * CAP + earlier)
        slot_s[i] = slots[i]
    for n in range(SLOTS):
        user = jnp.int32(tiles_dev)
        for i in range(tiles_dev):
            user = jnp.where(slots[i] == n, i, user)
        tile_s[n] = user
    before, ranks = jnp.int32(0), []
    for i in range(tiles_dev):
        own = dests[i] == 0
        ranks.append(jnp.where(own, slots[i], CAP + i - before))
        before = before + jnp.where(own, 1, 0)
        place_s[i] = ranks[i]
    for q in range(tiles_dev):
        user = jnp.int32(0)
        for i in range(tiles_dev):
            user = jnp.where(ranks[i] == q, i, user)
        perm_s[q] = user
    for i in range(tiles_dev):
        for r in range(blocks):
            rowmask[i * blocks + r] = jnp.where(row_in[i] == r, 1.0, 0.0).astype(F32)
    for n in range(SLOTS):
        for c in range(blocks):
            transmask[n * blocks + c] = jnp.where(trans_in[0, n] == c, 1.0, 0.0).astype(F32)
    terms[tiles_dev] = jnp.zeros_like(terms[tiles_dev])

    for load in loads:
        load.wait()
    for h in range(HB):
        b_fill(STEPS - 1, h)
    for h in range(HB):
        b_start(STEPS - 1, h)

    def g_copy(part, o):
        to = at_inj(o)
        span = pl.ds(CAP, tiles_dev - CAP) if part else pl.ds(0, CAP)
        return pltpu.make_async_remote_copy(
            gsend.at[to, span], grecv.at[o - 1, span], gs_sem.at[part, o - 1], gr_sem.at[part, o - 1],
            device_id=(to, me_b), device_id_type=MESH,
        )

    def gradient(part):
        for q in range(CAP, tiles_dev) if part else range(CAP):
            i = perm_s[q]
            slot = slot_s[i] if part else q
            columns = jnp.concatenate([fetched[t * HF + h][slot] for t in range(STEPS) for h in range(HF)], axis=0)
            full = dot_nn(adj_t[row_in[i]], columns) * (1.0 / sets)
            full = full.astype(BF16)
            for p in range(n_inj):
                gsend[p, q] = full[p * portion : (p + 1) * portion]
        for o in sorted(range(1, n_inj), key=lambda o: -min(o, n_inj - o)):
            g_copy(part, o).start()

    def g_sum(part):
        for o in range(1, n_inj):
            g_copy(part, o).wait_send()
            g_copy(part, o).wait_recv()
        span = pl.ds(CAP, tiles_dev - CAP) if part else pl.ds(0, CAP)
        mine = gsend[me_i, span].astype(F32)
        for o in range(1, n_inj):
            mine = mine + grecv[o - 1, span].astype(F32)
        gsum[span] = mine.astype(BF16)

    def transpose_pair(p):
        for r in range(blocks):
            both = adj[r, pl.ds(p * 2 * sets, 2 * sets)]
            adj_t[r, :, pl.ds(p * 2 * sets, 2 * sets)] = both.T

    def f_turn(k, h):
        if k:
            f_all(k - 1, h).wait_send()
        f_all(k, h).wait_recv()
        if k < STEPS - 1:
            f_step(k, h)
            f_fill(k + 1, h)
            f_start(k + 1, h)

    def b_turn(back, h):
        if back < STEPS - 1:
            b_all(back + 1, h).wait_send()
        b_all(back, h).wait_recv()
        total = b_step(back, h)
        for c in range(blocks):
            if back:
                adj[c, pl.ds((back - 1) * sets + h * bs, bs)] = total[c].astype(BF16)
            else:
                sens_ref[pl.ds(h * bs, bs), pl.ds(c * width, width)] = total[c].astype(BF16)
        if back:
            b_fill(back - 1, h)
            if back > 1:
                b_start(back - 1, h)

    for k in range(STEPS - 1):
        for h in range(HF):
            f_turn(k, h)
        for h in range(HB):
            b_turn(STEPS - 1 - k, h)
        if k == 0:
            transpose_pair(1)
        if k == STEPS - 2:
            transpose_pair(0)
            gradient(0)
    for h in range(HF):
        f_turn(STEPS - 1, h)
    for h in range(HB):
        b_start(0, h)
    gradient(1)
    for h in range(HB):
        b_turn(0, h)
    for h in range(HF):
        f_all(STEPS - 1, h).wait_send()
    for h in range(HB):
        b_all(0, h).wait_send()
    for part in range(2):
        g_sum(part)
    for i in range(tiles_dev):
        grad_ref[i] = gsum[place_s[i]]


def shards(tile_values, tile_row, tile_dest, trans_block, inj_pores, final_weight):
    tiles_dev, width = tile_values.shape[:2]
    sets, pores = final_weight.shape
    blocks = pores // width
    n_inj, n_blk = lax.axis_size("inj"), lax.axis_size("blk")
    portion = width // n_inj
    fs, bs = sets // HF, sets // HB
    vmem = pl.BlockSpec(memory_space=pltpu.VMEM)
    hbm = pl.BlockSpec(memory_space=pl.ANY)
    dma = pltpu.SemaphoreType.DMA
    return pl.pallas_call(
        functools.partial(sweep, n_inj, n_blk, blocks, tiles_dev),
        name="sweep",
        out_shape=(pltpu.VMEM((sets, pores), BF16), pltpu.VMEM((tiles_dev, portion, width), BF16)),
        in_specs=[hbm] * 6,
        out_specs=(vmem, vmem),
        scratch_shapes=[
            pltpu.SMEM((tiles_dev,), jnp.int32),
            pltpu.SMEM((tiles_dev,), jnp.int32),
            pltpu.SMEM(trans_block.shape, jnp.int32),
            pltpu.VMEM((tiles_dev, width, width), BF16),
            pltpu.VMEM(inj_pores.shape, jnp.int32),
            pltpu.VMEM((blocks, sets, width), BF16),
            pltpu.VMEM((blocks, STEPS * sets, width), BF16),
            pltpu.VMEM((blocks, width, STEPS * sets), BF16),
            pltpu.VMEM((tiles_dev + 1, bs, width), BF16),
            pltpu.VMEM((STEPS, HF, SLOTS, fs, width), BF16),
            pltpu.VMEM((STEPS, HB, SLOTS, bs, width), BF16),
            pltpu.VMEM((STEPS, HB, SLOTS, bs, width), BF16),
            pltpu.VMEM((n_inj, tiles_dev, portion, width), BF16),
            pltpu.VMEM((n_inj - 1, tiles_dev, portion, width), BF16),
            pltpu.VMEM((tiles_dev, portion, width), BF16),
            pltpu.SMEM((tiles_dev,), jnp.int32),
            pltpu.SMEM((SLOTS,), jnp.int32),
            pltpu.SMEM((tiles_dev,), jnp.int32),
            pltpu.SMEM((tiles_dev,), jnp.int32),
            pltpu.SMEM((tiles_dev * blocks,), F32),
            pltpu.SMEM((SLOTS * blocks,), F32),
            dma((5 + blocks,)),
            dma((STEPS, HF)),
            dma((STEPS, HF)),
            dma((STEPS, HB)),
            dma((STEPS, HB)),
            dma((2, n_inj - 1)),
            dma((2, n_inj - 1)),
        ]
        + [pltpu.VMEM((SLOTS, fs, width), BF16)] * (STEPS * HF),
        compiler_params=pltpu.CompilerParams(
            collective_id=0, has_side_effects=True, vmem_limit_bytes=60 * 1024 * 1024
        ),
    )(tile_row, tile_dest[:, 0], trans_block, tile_values, inj_pores, final_weight)


def solution(mesh):
    placed = (
        P("blk", None, None),
        P("blk"),
        P("blk", None),
        P("blk", None),
        P("inj", "blk"),
        P("inj", "blk"),
    )
    return jax.shard_map(
        shards,
        mesh=mesh,
        in_specs=placed,
        out_specs=(P("inj", "blk"), P("blk", "inj", None)),
        check_vma=False,
    )
```

```python
import functools

import jax
import jax.numpy as jnp
from jax import lax
from jax.experimental import pallas as pl
from jax.experimental.pallas import tpu as pltpu
from jax.sharding import PartitionSpec as P

NEIGH = 6
STEPS = 4
CAP = 3
SLOTS = (NEIGH + 1) * CAP
ORDER = (3, 4, 5, 6, 1, 2)
HF = 2
HB = 2
MESH = pl.DeviceIdType.MESH
F32 = jnp.float32
BF16 = jnp.bfloat16


def offset_of(slot):
    amount = (slot + 1) // 2
    return amount if slot % 2 == 1 else -amount


def dot_nt(x, y):
    return lax.dot_general(x, y, (((1,), (1,)), ((), ())), preferred_element_type=F32)


def dot_nn(x, y):
    return lax.dot_general(x, y, (((1,), (0,)), ((), ())), preferred_element_type=F32)


def sweep(
    n_inj, n_blk, blocks, tiles_dev, row_hbm, dest_hbm, trans_hbm, tiles_hbm, pores_hbm, weight_hbm,
    sens_ref, grad_ref, row_in, dest_in, trans_in, tiles, pores, state, adj, adj_t, terms, fsend, bsend, brecv, gsend, grecv,
    gsum, slot_s, tile_s, perm_s, place_s, rowmask, transmask, in_sem, fs_sem, fr_sem, bs_sem, br_sem, gs_sem, gr_sem, *fetched,
):
    me_i, me_b = lax.axis_index("inj"), lax.axis_index("blk")
    sets = pores.shape[0]
    fs, bs = sets // HF, sets // HB
    width = tiles.shape[-1]
    portion = width // n_inj

    def at_blk(distance):
        return (me_i, lax.rem(me_b + (distance + n_blk), n_blk))

    def at_inj(distance):
        return lax.rem(me_i + distance, n_inj)

    first = pltpu.make_async_copy(pores_hbm, pores, in_sem.at[0])
    first.start()
    barrier = pltpu.get_barrier_semaphore()
    for j in range(NEIGH, 0, -1):
        pl.semaphore_signal(barrier, inc=1, device_id=at_blk(offset_of(j)), device_id_type=MESH)
    for o in range(1, n_inj):
        pl.semaphore_signal(barrier, inc=1, device_id=(at_inj(o), me_b), device_id_type=MESH)

    small = [
        pltpu.make_async_copy(trans_hbm, trans_in, in_sem.at[2 + blocks]),
        pltpu.make_async_copy(row_hbm, row_in, in_sem.at[3 + blocks]),
        pltpu.make_async_copy(dest_hbm, dest_in, in_sem.at[4 + blocks]),
    ]
    loads = [
        pltpu.make_async_copy(tiles_hbm, tiles, in_sem.at[1]),
    ]
    for c in range(blocks):
        loads.append(
            pltpu.make_async_copy(
                weight_hbm.at[:, pl.ds(c * width, width)],
                adj.at[c, pl.ds((STEPS - 1) * sets, sets)],
                in_sem.at[2 + c],
            )
        )
    for load in small + loads:
        load.start()

    def f_copy(t, h, j, count=1):
        span = pl.ds(j * CAP, count * CAP)
        return pltpu.make_async_remote_copy(
            fsend.at[t, h, span], fetched[t * HF + h].at[span],
            fs_sem.at[t, h], fr_sem.at[t, h],
            device_id=at_blk(-offset_of(j)), device_id_type=MESH,
        )

    def b_copy(t, h, j, count=1):
        span = pl.ds(j * CAP, count * CAP)
        return pltpu.make_async_remote_copy(
            bsend.at[t, h, span], brecv.at[t, h, span],
            bs_sem.at[t, h], br_sem.at[t, h],
            device_id=at_blk(offset_of(j)), device_id_type=MESH,
        )

    def f_start(t, h):
        for j in ORDER:
            f_copy(t, h, j).start()

    def f_all(t, h):
        return f_copy(t, h, 1, NEIGH)

    def b_start(t, h):
        for j in ORDER:
            b_copy(t, h, j).start()

    def b_all(t, h):
        return b_copy(t, h, 1, NEIGH)

    def f_fill(t, h):
        for n in range(SLOTS):
            block = state[trans_in[0, n], pl.ds(h * fs, fs)]
            if n < CAP:
                fetched[t * HF + h][n] = block
            else:
                fsend[t, h, n] = block

    def b_fill(t, h):
        where = pl.ds(t * sets + h * bs, bs)
        for i in range(tiles_dev):
            terms[i] = dot_nn(adj[row_in[i], where], tiles[i]).astype(BF16)
        for n in range(SLOTS):
            block = terms[tile_s[n]]
            if n < CAP:
                brecv[t, h, n] = block
            else:
                bsend[t, h, n] = block

    def f_step(t, h):
        total = [None] * blocks
        for i in range(tiles_dev):
            part = dot_nt(fetched[t * HF + h][slot_s[i]], tiles[i])
            for r in range(blocks):
                kept = part * rowmask[i * blocks + r]
                total[r] = kept if total[r] is None else total[r] + kept
        for r in range(blocks):
            state[r, pl.ds(h * fs, fs)] = total[r].astype(BF16)

    def b_step(t, h):
        total = [None] * blocks
        for n in range(SLOTS):
            part = brecv[t, h, n].astype(F32)
            for c in range(blocks):
                kept = part * transmask[n * blocks + c]
                total[c] = kept if total[c] is None else total[c] + kept
        return total

    first.wait()
    ids = pores[...]
    low = lax.bitwise_and(ids, width - 1)
    unit = lax.shift_left(jnp.ones_like(ids), lax.shift_right_logical(ids, 7) * 8)
    lanes = lax.broadcasted_iota(jnp.int32, (sets, width), 1)
    counts = jnp.zeros((sets, width), jnp.int32)
    for e in range(ids.shape[1]):
        counts = counts + jnp.where(low[:, e : e + 1] == lanes, unit[:, e : e + 1], 0)
    for c in range(blocks):
        one = lax.bitwise_and(lax.shift_right_logical(counts, 8 * c), 255)
        state[c] = one.astype(F32).astype(BF16)
    small[0].wait()
    for h in range(HF):
        f_fill(0, h)
    pl.semaphore_wait(barrier, NEIGH + n_inj - 1)
    for h in range(HF):
        f_start(0, h)
    small[1].wait()
    small[2].wait()

    dests = [dest_in[i] for i in range(tiles_dev)]
    slots = []
    for i in range(tiles_dev):
        earlier = jnp.int32(0)
        for e in range(i):
            earlier = earlier + jnp.where(dests[e] == dests[i], 1, 0)
        slots.append(dests[i] * CAP + earlier)
        slot_s[i] = slots[i]
    for n in range(SLOTS):
        user = jnp.int32(tiles_dev)
        for i in range(tiles_dev):
            user = jnp.where(slots[i] == n, i, user)
        tile_s[n] = user
    before, ranks = jnp.int32(0), []
    for i in range(tiles_dev):
        own = dests[i] == 0
        ranks.append(jnp.where(own, slots[i], CAP + i - before))
        before = before + jnp.where(own, 1, 0)
        place_s[i] = ranks[i]
    for q in range(tiles_dev):
        user = jnp.int32(0)
        for i in range(tiles_dev):
            user = jnp.where(ranks[i] == q, i, user)
        perm_s[q] = user
    for i in range(tiles_dev):
        for r in range(blocks):
            rowmask[i * blocks + r] = jnp.where(row_in[i] == r, 1.0, 0.0).astype(F32)
    for n in range(SLOTS):
        for c in range(blocks):
            transmask[n * blocks + c] = jnp.where(trans_in[0, n] == c, 1.0, 0.0).astype(F32)
    terms[tiles_dev] = jnp.zeros_like(terms[tiles_dev])

    for load in loads:
        load.wait()
    for h in range(HB):
        b_fill(STEPS - 1, h)
    for h in range(HB):
        b_start(STEPS - 1, h)

    cuts = (0, CAP, (CAP + tiles_dev + 1) // 2, tiles_dev)

    def g_copy(part, o):
        to = at_inj(o)
        span = pl.ds(cuts[part], cuts[part + 1] - cuts[part])
        return pltpu.make_async_remote_copy(
            gsend.at[to, span], grecv.at[o - 1, span], gs_sem.at[part, o - 1], gr_sem.at[part, o - 1],
            device_id=(to, me_b), device_id_type=MESH,
        )

    def gradient(part):
        for q in range(cuts[part], cuts[part + 1]):
            i = perm_s[q]
            slot = slot_s[i] if part else q
            columns = jnp.concatenate([fetched[t * HF + h][slot] for t in range(STEPS) for h in range(HF)], axis=0)
            full = dot_nn(adj_t[row_in[i]], columns) * (1.0 / sets)
            full = full.astype(BF16)
            for p in range(n_inj):
                gsend[p, q] = full[p * portion : (p + 1) * portion]
        for o in sorted(range(1, n_inj), key=lambda o: -min(o, n_inj - o)):
            g_copy(part, o).start()

    def g_sum(part):
        for o in range(1, n_inj):
            g_copy(part, o).wait_send()
            g_copy(part, o).wait_recv()
        span = pl.ds(cuts[part], cuts[part + 1] - cuts[part])
        mine = gsend[me_i, span].astype(F32)
        for o in range(1, n_inj):
            mine = mine + grecv[o - 1, span].astype(F32)
        gsum[span] = mine.astype(BF16)

    def transpose_pair(p):
        for r in range(blocks):
            both = adj[r, pl.ds(p * 2 * sets, 2 * sets)]
            adj_t[r, :, pl.ds(p * 2 * sets, 2 * sets)] = both.T

    def f_turn(k, h):
        if k:
            f_all(k - 1, h).wait_send()
        f_all(k, h).wait_recv()
        if k < STEPS - 1:
            f_step(k, h)
            f_fill(k + 1, h)
            f_start(k + 1, h)

    def b_turn(back, h):
        if back < STEPS - 1:
            b_all(back + 1, h).wait_send()
        b_all(back, h).wait_recv()
        total = b_step(back, h)
        for c in range(blocks):
            if back:
                adj[c, pl.ds((back - 1) * sets + h * bs, bs)] = total[c].astype(BF16)
            else:
                sens_ref[pl.ds(h * bs, bs), pl.ds(c * width, width)] = total[c].astype(BF16)
        if back:
            b_fill(back - 1, h)
            if back > 1:
                b_start(back - 1, h)

    for k in range(STEPS - 1):
        for h in range(HF):
            f_turn(k, h)
        for h in range(HB):
            b_turn(STEPS - 1 - k, h)
        if k == 0:
            transpose_pair(1)
        if k == STEPS - 2:
            transpose_pair(0)
            gradient(0)
    for h in range(HF):
        f_turn(STEPS - 1, h)
    for h in range(HB):
        b_start(0, h)
    gradient(1)
    gradient(2)
    g_sum(0)
    for h in range(HB):
        b_turn(0, h)
    for h in range(HF):
        f_all(STEPS - 1, h).wait_send()
    for h in range(HB):
        b_all(0, h).wait_send()
    g_sum(1)
    g_sum(2)
    for i in range(tiles_dev):
        grad_ref[i] = gsum[place_s[i]]


def shards(tile_values, tile_row, tile_dest, trans_block, inj_pores, final_weight):
    tiles_dev, width = tile_values.shape[:2]
    sets, pores = final_weight.shape
    blocks = pores // width
    n_inj, n_blk = lax.axis_size("inj"), lax.axis_size("blk")
    portion = width // n_inj
    fs, bs = sets // HF, sets // HB
    vmem = pl.BlockSpec(memory_space=pltpu.VMEM)
    hbm = pl.BlockSpec(memory_space=pl.ANY)
    dma = pltpu.SemaphoreType.DMA
    return pl.pallas_call(
        functools.partial(sweep, n_inj, n_blk, blocks, tiles_dev),
        name="sweep",
        out_shape=(pltpu.VMEM((sets, pores), BF16), pltpu.VMEM((tiles_dev, portion, width), BF16)),
        in_specs=[hbm] * 6,
        out_specs=(vmem, vmem),
        scratch_shapes=[
            pltpu.SMEM((tiles_dev,), jnp.int32),
            pltpu.SMEM((tiles_dev,), jnp.int32),
            pltpu.SMEM(trans_block.shape, jnp.int32),
            pltpu.VMEM((tiles_dev, width, width), BF16),
            pltpu.VMEM(inj_pores.shape, jnp.int32),
            pltpu.VMEM((blocks, sets, width), BF16),
            pltpu.VMEM((blocks, STEPS * sets, width), BF16),
            pltpu.VMEM((blocks, width, STEPS * sets), BF16),
            pltpu.VMEM((tiles_dev + 1, bs, width), BF16),
            pltpu.VMEM((STEPS, HF, SLOTS, fs, width), BF16),
            pltpu.VMEM((STEPS, HB, SLOTS, bs, width), BF16),
            pltpu.VMEM((STEPS, HB, SLOTS, bs, width), BF16),
            pltpu.VMEM((n_inj, tiles_dev, portion, width), BF16),
            pltpu.VMEM((n_inj - 1, tiles_dev, portion, width), BF16),
            pltpu.VMEM((tiles_dev, portion, width), BF16),
            pltpu.SMEM((tiles_dev,), jnp.int32),
            pltpu.SMEM((SLOTS,), jnp.int32),
            pltpu.SMEM((tiles_dev,), jnp.int32),
            pltpu.SMEM((tiles_dev,), jnp.int32),
            pltpu.SMEM((tiles_dev * blocks,), F32),
            pltpu.SMEM((SLOTS * blocks,), F32),
            dma((5 + blocks,)),
            dma((STEPS, HF)),
            dma((STEPS, HF)),
            dma((STEPS, HB)),
            dma((STEPS, HB)),
            dma((3, n_inj - 1)),
            dma((3, n_inj - 1)),
        ]
        + [pltpu.VMEM((SLOTS, fs, width), BF16)] * (STEPS * HF),
        compiler_params=pltpu.CompilerParams(
            collective_id=0, has_side_effects=True, vmem_limit_bytes=60 * 1024 * 1024
        ),
    )(tile_row, tile_dest[:, 0], trans_block, tile_values, inj_pores, final_weight)


def solution(mesh):
    placed = (
        P("blk", None, None),
        P("blk"),
        P("blk", None),
        P("blk", None),
        P("inj", "blk"),
        P("inj", "blk"),
    )
    return jax.shard_map(
        shards,
        mesh=mesh,
        in_specs=placed,
        out_specs=(P("inj", "blk"), P("blk", "inj", None)),
        check_vma=False,
    )
```

```python
import functools

import jax
import jax.numpy as jnp
from jax import lax
from jax.experimental import pallas as pl
from jax.experimental.pallas import tpu as pltpu
from jax.sharding import PartitionSpec as P

NEIGH = 6
STEPS = 4
CAP = 3
SLOTS = (NEIGH + 1) * CAP
ORDER = (1, 2, 3, 4, 5, 6)
HF = 2
HB = 2
MESH = pl.DeviceIdType.MESH
F32 = jnp.float32
BF16 = jnp.bfloat16


def offset_of(slot):
    amount = (slot + 1) // 2
    return amount if slot % 2 == 1 else -amount


def dot_nt(x, y):
    return lax.dot_general(x, y, (((1,), (1,)), ((), ())), preferred_element_type=F32)


def dot_nn(x, y):
    return lax.dot_general(x, y, (((1,), (0,)), ((), ())), preferred_element_type=F32)


def sweep(
    n_inj, n_blk, blocks, tiles_dev, row_hbm, dest_hbm, trans_hbm, tiles_hbm, pores_hbm, weight_hbm,
    sens_ref, grad_ref, row_in, dest_in, trans_in, tiles, pores, state, adj, adj_t, terms, fsend, bsend, brecv, gsend, grecv,
    gsum, slot_s, tile_s, perm_s, place_s, rowmask, transmask, in_sem, fs_sem, fr_sem, bs_sem, br_sem, gs_sem, gr_sem, *fetched,
):
    me_i, me_b = lax.axis_index("inj"), lax.axis_index("blk")
    sets = pores.shape[0]
    fs, bs = sets // HF, sets // HB
    width = tiles.shape[-1]
    portion = width // n_inj

    def at_blk(distance):
        return (me_i, lax.rem(me_b + (distance + n_blk), n_blk))

    def at_inj(distance):
        return lax.rem(me_i + distance, n_inj)

    first = pltpu.make_async_copy(pores_hbm, pores, in_sem.at[0])
    first.start()
    barrier = pltpu.get_barrier_semaphore()
    for j in range(NEIGH, 0, -1):
        pl.semaphore_signal(barrier, inc=1, device_id=at_blk(offset_of(j)), device_id_type=MESH)
    for o in range(1, n_inj):
        pl.semaphore_signal(barrier, inc=1, device_id=(at_inj(o), me_b), device_id_type=MESH)

    small = [
        pltpu.make_async_copy(trans_hbm, trans_in, in_sem.at[2 + blocks]),
        pltpu.make_async_copy(row_hbm, row_in, in_sem.at[3 + blocks]),
        pltpu.make_async_copy(dest_hbm, dest_in, in_sem.at[4 + blocks]),
    ]
    loads = [
        pltpu.make_async_copy(tiles_hbm, tiles, in_sem.at[1]),
    ]
    for c in range(blocks):
        loads.append(
            pltpu.make_async_copy(
                weight_hbm.at[:, pl.ds(c * width, width)],
                adj.at[c, pl.ds((STEPS - 1) * sets, sets)],
                in_sem.at[2 + c],
            )
        )
    for load in small + loads:
        load.start()

    def f_copy(t, h, j, count=1):
        span = pl.ds(j * CAP, count * CAP)
        return pltpu.make_async_remote_copy(
            fsend.at[t, h, span], fetched[t * HF + h].at[span],
            fs_sem.at[t, h], fr_sem.at[t, h],
            device_id=at_blk(-offset_of(j)), device_id_type=MESH,
        )

    def b_copy(t, h, j, count=1):
        span = pl.ds(j * CAP, count * CAP)
        return pltpu.make_async_remote_copy(
            bsend.at[t, h, span], brecv.at[t, h, span],
            bs_sem.at[t, h], br_sem.at[t, h],
            device_id=at_blk(offset_of(j)), device_id_type=MESH,
        )

    def f_start(t, h):
        for j in ORDER:
            f_copy(t, h, j).start()

    def f_all(t, h):
        return f_copy(t, h, 1, NEIGH)

    def b_start(t, h):
        for j in ORDER:
            b_copy(t, h, j).start()

    def b_all(t, h):
        return b_copy(t, h, 1, NEIGH)

    def f_fill(t, h):
        for n in range(SLOTS):
            block = state[trans_in[0, n], pl.ds(h * fs, fs)]
            if n < CAP:
                fetched[t * HF + h][n] = block
            else:
                fsend[t, h, n] = block

    def b_fill(t, h):
        where = pl.ds(t * sets + h * bs, bs)
        for i in range(tiles_dev):
            terms[i] = dot_nn(adj[row_in[i], where], tiles[i]).astype(BF16)
        for n in range(SLOTS):
            block = terms[tile_s[n]]
            if n < CAP:
                brecv[t, h, n] = block
            else:
                bsend[t, h, n] = block

    def f_step(t, h):
        total = [None] * blocks
        for i in range(tiles_dev):
            part = dot_nt(fetched[t * HF + h][slot_s[i]], tiles[i])
            for r in range(blocks):
                kept = part * rowmask[i * blocks + r]
                total[r] = kept if total[r] is None else total[r] + kept
        for r in range(blocks):
            state[r, pl.ds(h * fs, fs)] = total[r].astype(BF16)

    def b_step(t, h):
        total = [None] * blocks
        for n in range(SLOTS):
            part = brecv[t, h, n].astype(F32)
            for c in range(blocks):
                kept = part * transmask[n * blocks + c]
                total[c] = kept if total[c] is None else total[c] + kept
        return total

    first.wait()
    ids = pores[...]
    low = lax.bitwise_and(ids, width - 1)
    unit = lax.shift_left(jnp.ones_like(ids), lax.shift_right_logical(ids, 7) * 8)
    lanes = lax.broadcasted_iota(jnp.int32, (sets, width), 1)
    counts = jnp.zeros((sets, width), jnp.int32)
    for e in range(ids.shape[1]):
        counts = counts + jnp.where(low[:, e : e + 1] == lanes, unit[:, e : e + 1], 0)
    for c in range(blocks):
        one = lax.bitwise_and(lax.shift_right_logical(counts, 8 * c), 255)
        state[c] = one.astype(F32).astype(BF16)
    small[0].wait()
    for h in range(HF):
        f_fill(0, h)
    pl.semaphore_wait(barrier, NEIGH + n_inj - 1)
    for h in range(HF):
        f_start(0, h)
    small[1].wait()
    small[2].wait()

    dests = [dest_in[i] for i in range(tiles_dev)]
    slots = []
    for i in range(tiles_dev):
        earlier = jnp.int32(0)
        for e in range(i):
            earlier = earlier + jnp.where(dests[e] == dests[i], 1, 0)
        slots.append(dests[i] * CAP + earlier)
        slot_s[i] = slots[i]
    for n in range(SLOTS):
        user = jnp.int32(tiles_dev)
        for i in range(tiles_dev):
            user = jnp.where(slots[i] == n, i, user)
        tile_s[n] = user
    before, ranks = jnp.int32(0), []
    for i in range(tiles_dev):
        own = dests[i] == 0
        ranks.append(jnp.where(own, slots[i], CAP + i - before))
        before = before + jnp.where(own, 1, 0)
        place_s[i] = ranks[i]
    for q in range(tiles_dev):
        user = jnp.int32(0)
        for i in range(tiles_dev):
            user = jnp.where(ranks[i] == q, i, user)
        perm_s[q] = user
    for i in range(tiles_dev):
        for r in range(blocks):
            rowmask[i * blocks + r] = jnp.where(row_in[i] == r, 1.0, 0.0).astype(F32)
    for n in range(SLOTS):
        for c in range(blocks):
            transmask[n * blocks + c] = jnp.where(trans_in[0, n] == c, 1.0, 0.0).astype(F32)
    terms[tiles_dev] = jnp.zeros_like(terms[tiles_dev])

    for load in loads:
        load.wait()
    for h in range(HB):
        b_fill(STEPS - 1, h)
    for h in range(HB):
        b_start(STEPS - 1, h)

    cuts = (0, CAP, (CAP + tiles_dev + 1) // 2, tiles_dev)

    def g_copy(part, o):
        to = at_inj(o)
        span = pl.ds(cuts[part], cuts[part + 1] - cuts[part])
        return pltpu.make_async_remote_copy(
            gsend.at[to, span], grecv.at[o - 1, span], gs_sem.at[part, o - 1], gr_sem.at[part, o - 1],
            device_id=(to, me_b), device_id_type=MESH,
        )

    def gradient(part):
        for q in range(cuts[part], cuts[part + 1]):
            i = perm_s[q]
            slot = slot_s[i] if part else q
            columns = jnp.concatenate([fetched[t * HF + h][slot] for t in range(STEPS) for h in range(HF)], axis=0)
            full = dot_nn(adj_t[row_in[i]], columns) * (1.0 / sets)
            full = full.astype(BF16)
            for p in range(n_inj):
                gsend[p, q] = full[p * portion : (p + 1) * portion]
        for o in sorted(range(1, n_inj), key=lambda o: -min(o, n_inj - o)):
            g_copy(part, o).start()

    def g_sum(part):
        for o in range(1, n_inj):
            g_copy(part, o).wait_send()
            g_copy(part, o).wait_recv()
        span = pl.ds(cuts[part], cuts[part + 1] - cuts[part])
        mine = gsend[me_i, span].astype(F32)
        for o in range(1, n_inj):
            mine = mine + grecv[o - 1, span].astype(F32)
        gsum[span] = mine.astype(BF16)

    def transpose_pair(p):
        for r in range(blocks):
            both = adj[r, pl.ds(p * 2 * sets, 2 * sets)]
            adj_t[r, :, pl.ds(p * 2 * sets, 2 * sets)] = both.T

    def f_turn(k, h):
        if k:
            f_all(k - 1, h).wait_send()
        f_all(k, h).wait_recv()
        if k < STEPS - 1:
            f_step(k, h)
            f_fill(k + 1, h)
            f_start(k + 1, h)

    def b_turn(back, h):
        if back < STEPS - 1:
            b_all(back + 1, h).wait_send()
        b_all(back, h).wait_recv()
        total = b_step(back, h)
        for c in range(blocks):
            if back:
                adj[c, pl.ds((back - 1) * sets + h * bs, bs)] = total[c].astype(BF16)
            else:
                sens_ref[pl.ds(h * bs, bs), pl.ds(c * width, width)] = total[c].astype(BF16)
        if back:
            b_fill(back - 1, h)
            if back > 1:
                b_start(back - 1, h)

    for k in range(STEPS - 1):
        for h in range(HF):
            f_turn(k, h)
        for h in range(HB):
            b_turn(STEPS - 1 - k, h)
        if k == 0:
            transpose_pair(1)
        if k == STEPS - 2:
            transpose_pair(0)
            gradient(0)
    for h in range(HF):
        f_turn(STEPS - 1, h)
    for h in range(HB):
        b_start(0, h)
    gradient(1)
    gradient(2)
    g_sum(0)
    for h in range(HB):
        b_turn(0, h)
    for h in range(HF):
        f_all(STEPS - 1, h).wait_send()
    for h in range(HB):
        b_all(0, h).wait_send()
    g_sum(1)
    g_sum(2)
    for i in range(tiles_dev):
        grad_ref[i] = gsum[place_s[i]]


def shards(tile_values, tile_row, tile_dest, trans_block, inj_pores, final_weight):
    tiles_dev, width = tile_values.shape[:2]
    sets, pores = final_weight.shape
    blocks = pores // width
    n_inj, n_blk = lax.axis_size("inj"), lax.axis_size("blk")
    portion = width // n_inj
    fs, bs = sets // HF, sets // HB
    vmem = pl.BlockSpec(memory_space=pltpu.VMEM)
    hbm = pl.BlockSpec(memory_space=pl.ANY)
    dma = pltpu.SemaphoreType.DMA
    return pl.pallas_call(
        functools.partial(sweep, n_inj, n_blk, blocks, tiles_dev),
        name="sweep",
        out_shape=(pltpu.VMEM((sets, pores), BF16), pltpu.VMEM((tiles_dev, portion, width), BF16)),
        in_specs=[hbm] * 6,
        out_specs=(vmem, vmem),
        scratch_shapes=[
            pltpu.SMEM((tiles_dev,), jnp.int32),
            pltpu.SMEM((tiles_dev,), jnp.int32),
            pltpu.SMEM(trans_block.shape, jnp.int32),
            pltpu.VMEM((tiles_dev, width, width), BF16),
            pltpu.VMEM(inj_pores.shape, jnp.int32),
            pltpu.VMEM((blocks, sets, width), BF16),
            pltpu.VMEM((blocks, STEPS * sets, width), BF16),
            pltpu.VMEM((blocks, width, STEPS * sets), BF16),
            pltpu.VMEM((tiles_dev + 1, bs, width), BF16),
            pltpu.VMEM((STEPS, HF, SLOTS, fs, width), BF16),
            pltpu.VMEM((STEPS, HB, SLOTS, bs, width), BF16),
            pltpu.VMEM((STEPS, HB, SLOTS, bs, width), BF16),
            pltpu.VMEM((n_inj, tiles_dev, portion, width), BF16),
            pltpu.VMEM((n_inj - 1, tiles_dev, portion, width), BF16),
            pltpu.VMEM((tiles_dev, portion, width), BF16),
            pltpu.SMEM((tiles_dev,), jnp.int32),
            pltpu.SMEM((SLOTS,), jnp.int32),
            pltpu.SMEM((tiles_dev,), jnp.int32),
            pltpu.SMEM((tiles_dev,), jnp.int32),
            pltpu.SMEM((tiles_dev * blocks,), F32),
            pltpu.SMEM((SLOTS * blocks,), F32),
            dma((5 + blocks,)),
            dma((STEPS, HF)),
            dma((STEPS, HF)),
            dma((STEPS, HB)),
            dma((STEPS, HB)),
            dma((3, n_inj - 1)),
            dma((3, n_inj - 1)),
        ]
        + [pltpu.VMEM((SLOTS, fs, width), BF16)] * (STEPS * HF),
        compiler_params=pltpu.CompilerParams(
            collective_id=0, has_side_effects=True, vmem_limit_bytes=60 * 1024 * 1024
        ),
    )(tile_row, tile_dest[:, 0], trans_block, tile_values, inj_pores, final_weight)


def solution(mesh):
    placed = (
        P("blk", None, None),
        P("blk"),
        P("blk", None),
        P("blk", None),
        P("inj", "blk"),
        P("inj", "blk"),
    )
    return jax.shard_map(
        shards,
        mesh=mesh,
        in_specs=placed,
        out_specs=(P("inj", "blk"), P("blk", "inj", None)),
        check_vma=False,
    )
```
